128 devices in a mesh: dp: 32 (over y, z, x_hi), tensor: 4 (over x_lo, core).
Axes of the slice: x: 4 (x_hi: 2, x_lo: 2; x = x_hi * 2 + x_lo), y: 4, z: 4, core: 2. Of those that a mesh axis runs over, the one named last changes fastest.
Arguments:
- tokens: bfloat16 [16384, 2048], P(('dp', 'tensor')), may hold values from -6 to 6
- segment_ids: int32 [16384], P('dp'), may hold values from 0 to 254, as said below
- norm1_gain: float32 [2048], replicated, may hold values from 0.5 to 1.5
- norm1_shift: float32 [2048], replicated, may hold values from -3 to 3
- w_query: bfloat16 [2048, 2048], P(None, 'tensor'), may hold values from -0.125 to 0.125
- w_key: bfloat16 [2048, 2048], P(None, 'tensor'), may hold values from -0.125 to 0.125
- w_value: bfloat16 [2048, 4096], P(None, 'tensor'), may hold values from -0.125 to 0.125
- w_gate: bfloat16 [2048, 4096], P(None, 'tensor'), may hold values from -0.125 to 0.125
- w_output: bfloat16 [4096, 2048], P('tensor'), may hold values from -0.09375 to 0.09375
- norm2_gain: float32 [2048], replicated, may hold values from 0.5 to 1.5
- norm2_shift: float32 [2048], replicated, may hold values from -3 to 3
- w_up: bfloat16 [2048, 4096], P(None, 'tensor'), may hold values from -0.125 to 0.125
- w_down: bfloat16 [4096, 2048], P('tensor'), may hold values from -0.09375 to 0.09375
- cotangent: bfloat16 [16384, 2048], P(('dp', 'tensor')), may hold values from -6 to 6
Outputs:
- block_out: bfloat16 [16384, 2048], P(('dp', 'tensor'))
- tokens_grad: float32 [16384, 2048], P(('dp', 'tensor'))
- norm1_gain_grad: float32 [2048], P(('dp', 'tensor'))
- norm1_shift_grad: float32 [2048], P(('dp', 'tensor'))
- query_grad: float32 [2048, 2048], P('dp', 'tensor')
- key_grad: float32 [2048, 2048], P('dp', 'tensor')
- value_grad: float32 [2048, 4096], P('dp', 'tensor')
- gate_grad: float32 [2048, 4096], P('dp', 'tensor')
- output_grad: float32 [4096, 2048], P('tensor', 'dp')
- norm2_gain_grad: float32 [2048], P(('dp', 'tensor'))
- norm2_shift_grad: float32 [2048], P(('dp', 'tensor'))
- up_grad: float32 [2048, 4096], P('dp', 'tensor')
- down_grad: float32 [4096, 2048], P('tensor', 'dp')
The draws below stay inside these ranges and needn't reach their ends.
Inputs may be any that keep to these rules, and one draw needn't show every extreme that they name: `segment_ids`: within each packed row of 512 positions the ids never fall; rows have disjoint ids; row r's ids start at 8 * r; three document boundaries lie in the row's first eighth of positions and three in its last eighth (they may coincide), so one document spans the middle of every row.
All inputs are finite; a program needn't handle non-finite values.
Results may differ from the reference program's by a relative error of at most 0.025.
Values may be sent and summed in bfloat16 or wider, within the bound.
No kernel may reach another device: no remote copies, remote signals or barrier semaphores. Data moves between devices by JAX's collectives and lax.ppermute only.
A program may use at most 192 MiB of HBM per device.

```python
import jax
import jax.numpy as jnp
from jax import lax

D = 2048
H = 8
DK = 256
DV = 512
FF = 4096
LEN = 512
QK = 2048
VD = 4096
TOKENS = 16384
N_DP = 32


def draw_segment_ids(key, part):
    key = jax.random.fold_in(key, 7)
    front_key, back_key = jax.random.split(key)
    eighth = max(LEN // 8, 1)
    front = jax.random.randint(front_key, (N_DP, 3), 1, eighth + 1)
    back = jax.random.randint(back_key, (N_DP, 3), LEN - eighth, LEN)
    cuts = jnp.concatenate([front, back], axis=1)
    position = jnp.arange(LEN, dtype=jnp.int32)
    local_ids = jnp.sum((position[None, :, None] >= cuts[:, None, :]).astype(jnp.int32), axis=2)
    row_base = 8 * jnp.arange(N_DP, dtype=jnp.int32)[:, None]
    return (local_ids + row_base).reshape(N_DP * LEN).astype(jnp.int32)


def levels(key, dims, cuts, least, high):
    level = 1.0
    for dim, parts in cuts:
        steps = jax.random.uniform(jax.random.fold_in(jax.random.fold_in(key, 6), dim), (parts,), jnp.float32, least / len(cuts), high / len(cuts))
        level = level * jnp.repeat(jnp.exp(steps), dims[dim] // parts).reshape((-1,) + (1,) * (len(dims) - 1 - dim))
    return level


def gaussian(stream_key, shape, scale, bound, shards=(), held_as=jnp.bfloat16):
    level = levels(stream_key, shape, shards, -0.22, 0.18) if shards else 1.0
    entries = jax.random.normal(stream_key, shape, jnp.float32) * scale * level
    return jnp.minimum(jnp.maximum(entries, -bound), bound).astype(held_as)


def setup_inputs(seed: int = 0) -> dict:
    seeds = jax.random.split(jax.random.key(seed), 15)
    tokens = gaussian(seeds[0], (TOKENS, D), 1.0, 6.0, ((0, 128),))
    segment_ids = draw_segment_ids(jax.random.fold_in(seeds[14], 71), 0)
    norm1_gain = jnp.clip(1.0 + 0.1 * jax.random.normal(seeds[2], (D,), jnp.float32), 0.5, 1.5)
    norm1_shift = gaussian(seeds[3], (D,), 0.5, 3.0, (), jnp.float32)
    w_query = gaussian(seeds[4], (D, QK), D ** -0.5, 0.125, ((1, 4),))
    w_key = gaussian(seeds[5], (D, QK), D ** -0.5, 0.125, ((1, 4),))
    w_value = gaussian(seeds[6], (D, VD), D ** -0.5, 0.125, ((1, 4),))
    w_gate = gaussian(seeds[7], (D, VD), D ** -0.5, 0.125, ((1, 4),))
    w_output = gaussian(seeds[8], (VD, D), VD ** -0.5, 0.09375, ((0, 4),))
    norm2_gain = jnp.clip(1.0 + 0.1 * jax.random.normal(seeds[9], (D,), jnp.float32), 0.5, 1.5)
    norm2_shift = gaussian(seeds[10], (D,), 0.5, 3.0, (), jnp.float32)
    w_up = gaussian(seeds[11], (D, FF), D ** -0.5, 0.125, ((1, 4),))
    w_down = gaussian(seeds[12], (FF, D), FF ** -0.5, 0.09375, ((0, 4),))
    cotangent = gaussian(seeds[13], (TOKENS, D), 1.0, 6.0, ((0, 128),))
    return dict(tokens=tokens, segment_ids=segment_ids, norm1_gain=norm1_gain, norm1_shift=norm1_shift, w_query=w_query, w_key=w_key, w_value=w_value, w_gate=w_gate, w_output=w_output, norm2_gain=norm2_gain, norm2_shift=norm2_shift, w_up=w_up, w_down=w_down, cotangent=cotangent)


@jax.custom_vjp
def low(v):
    return lax.optimization_barrier(v.astype(jnp.bfloat16)).astype(jnp.float32)

@jax.custom_vjp
def low_back(v):
    return v

def low_keep(v):
    return (low(v), None)

def low_pass(kept, grad):
    return (grad,)

def back_keep(v):
    return (v, None)

def back_low(kept, grad):
    return (low(grad),)
low.defvjp(low_keep, low_pass)
low_back.defvjp(back_keep, back_low)

def product(left, right):
    return jnp.dot(left, right, precision=lax.Precision.HIGHEST)

def layer_norm(value, gain, shift):
    centred = value - lax.optimization_barrier(jnp.mean(value, axis=-1, keepdims=True))
    spread = lax.optimization_barrier(jnp.mean(centred * centred, axis=-1, keepdims=True))
    return centred * lax.rsqrt(spread + 1e-05) * gain + shift

def rotate(value, head_count, turn):
    length = value.shape[0]
    half = DK // 2
    freqs = 10000.0 ** (-jnp.arange(half, dtype=jnp.float32) / half)
    angle = jnp.arange(length, dtype=jnp.float32)[:, None] * freqs[None, :]
    cosine = jnp.cos(angle)[:, None, :]
    sine = turn * jnp.sin(angle)[:, None, :]
    split = value.reshape(length, head_count, 2, half)
    first = split[:, :, 0]
    second = split[:, :, 1]
    joined = jnp.concatenate([first * cosine - second * sine, first * sine + second * cosine], axis=-1)
    return joined.reshape(length, head_count * DK)

def decay_table(segment, first_head, head_count):
    length = segment.shape[0]
    position = jnp.arange(length, dtype=jnp.int32)
    distance = position[:, None] - position[None, :]
    allowed = (segment[:, None] == segment[None, :]) & (distance >= 0)
    head_ids = (first_head + jnp.arange(head_count, dtype=jnp.int32)).astype(jnp.float32)
    rate = jnp.log(1.0 - 2.0 ** (-5.0 - head_ids))
    steps_back = jnp.where(allowed, distance, jnp.zeros_like(distance)).astype(jnp.float32)
    return jnp.where(allowed[None], jnp.exp(steps_back[None] * rate[:, None, None]), 0.0)

def forward(tokens, segment, norm1_gain, norm1_shift, w_query, w_key, w_value, w_gate, w_output, norm2_gain, norm2_shift, w_up, w_down):
    length = tokens.shape[0]
    hidden1 = low(layer_norm(tokens, norm1_gain, norm1_shift))
    query_matrix = low(rotate(low_back(product(hidden1, w_query)), H, 1.0)).reshape(length, H, DK)
    key_matrix = low(rotate(low_back(product(hidden1, w_key)), H, 1.0)).reshape(length, H, DK)
    value_matrix = low(low_back(product(hidden1, w_value))).reshape(length, H, DV)
    gate_pre = low_back(product(hidden1, w_gate))
    unmasked_scores = low_back(jnp.einsum('vqj,fqj->qvf', query_matrix, key_matrix, precision=lax.Precision.HIGHEST))
    decayed_scores = low(unmasked_scores * DK ** (-0.5) * decay_table(segment, 0, H))
    mixed_values = low_back(jnp.einsum('fkg,gfy->kfy', decayed_scores, value_matrix, precision=lax.Precision.HIGHEST))
    centred = mixed_values - lax.optimization_barrier(jnp.mean(mixed_values, axis=-1, keepdims=True))
    group_normed = centred * lax.rsqrt(lax.optimization_barrier(jnp.mean(centred * centred, axis=-1, keepdims=True)) + 1.0)
    gated = low(jax.nn.silu(gate_pre) * group_normed.reshape(length, H * DV))
    mid_rows = tokens + low_back(product(gated, w_output))
    hidden2 = low(layer_norm(mid_rows, norm2_gain, norm2_shift))
    up_pre = low_back(product(hidden2, w_up))
    activated = low(jax.nn.gelu(up_pre, approximate=True))
    return mid_rows + low_back(product(activated, w_down))

def reference(tokens, segment_ids, norm1_gain, norm1_shift, w_query, w_key, w_value, w_gate, w_output, norm2_gain, norm2_shift, w_up, w_down, cotangent):
    params = (norm1_gain.astype(jnp.float32), norm1_shift.astype(jnp.float32), w_query.astype(jnp.float32), w_key.astype(jnp.float32), w_value.astype(jnp.float32), w_gate.astype(jnp.float32), w_output.astype(jnp.float32), norm2_gain.astype(jnp.float32), norm2_shift.astype(jnp.float32), w_up.astype(jnp.float32), w_down.astype(jnp.float32))
    row_inputs = tokens.astype(jnp.float32).reshape(N_DP, LEN, D)
    row_segments = segment_ids.reshape(N_DP, LEN)
    row_cotangents = cotangent.astype(jnp.float32).reshape(N_DP, LEN, D)

    def one_row(carry, item):
        inputs, segment, cotan = item

        def apply(inputs_now, *weights):
            return forward(inputs_now, segment, *weights)
        output, pull = jax.vjp(apply, inputs, *params)
        grads = pull(cotan)
        carry = tuple((total + part for total, part in zip(carry, grads[1:])))
        return (carry, (output.astype(jnp.bfloat16), grads[0]))
    zeros = tuple((jnp.zeros_like(weight) for weight in params))
    sums, (outputs, input_grads) = lax.scan(one_row, zeros, (row_inputs, row_segments, row_cotangents))
    return (outputs.reshape(TOKENS, D), input_grads.reshape(TOKENS, D), sums[0], sums[1], sums[2], sums[3], sums[4], sums[5], sums[6], sums[7], sums[8], sums[9], sums[10])
```

```python
import jax
import jax.numpy as jnp
from jax import lax
from jax.sharding import PartitionSpec as P

H = 8
DK = 256
DV = 512
F32 = jnp.float32
BF = jnp.bfloat16
SHIFTS = (1, -1, 2)


def shift_y(value, step):
    return lax.ppermute(
        value, "dp", [(i, ((i // 8 + step) % 4) * 8 + i % 8) for i in range(32)]
    )


def shift_z(value, step):
    return lax.ppermute(
        value,
        "dp",
        [(i, (i // 8) * 8 + ((i // 2 % 4 + step) % 4) * 2 + i % 2) for i in range(32)],
    )


def swap_xh(value):
    return lax.ppermute(value, "dp", [(i, i ^ 1) for i in range(32)])


def swap_xl(value):
    return lax.ppermute(value, "tensor", [(i, i ^ 2) for i in range(4)])


def swap_core(value):
    return lax.ppermute(value, "tensor", [(i, i ^ 1) for i in range(4)])


def gather_row(own):
    across = swap_xl(own)
    return jnp.concatenate([own, across, swap_core(own), swap_core(across)], axis=0)


def scatter_row(parts, wide):
    quarter = parts.shape[0] // 4
    far = parts[quarter : 2 * quarter] + swap_core(parts[3 * quarter :].astype(wide)).astype(F32)
    near = parts[:quarter] + swap_core(parts[2 * quarter : 3 * quarter].astype(wide)).astype(F32)
    return near + swap_xl(far.astype(BF)).astype(F32)


def dot(left, right):
    return jnp.dot(left, right, preferred_element_type=F32)


def dot_tn(left, right):
    return lax.dot_general(left, right, (((0,), (0,)), ((), ())), preferred_element_type=F32)


def dot_nt(left, right):
    return lax.dot_general(left, right, (((1,), (1,)), ((), ())), preferred_element_type=F32)


def norm_rows(value, epsilon):
    centred = value - jnp.mean(value, axis=-1, keepdims=True)
    factor = lax.rsqrt(jnp.mean(centred * centred, axis=-1, keepdims=True) + epsilon)
    return (centred * factor, factor)


def norm_back(grad, normed, factor):
    return factor * (
        grad
        - jnp.mean(grad, axis=-1, keepdims=True)
        - normed * jnp.mean(grad * normed, axis=-1, keepdims=True)
    )


def rotate(value, cosine, sine):
    half = DK // 2
    first = value[:, :half]
    second = value[:, half:]
    return jnp.concatenate(
        [first * cosine - second * sine, first * sine + second * cosine], axis=-1
    )


def piece(value, index, size, axis):
    return lax.dynamic_slice_in_dim(value, index * size, size, axis)


def model_slice(value, index, along):
    if along == "y":
        return piece(value, index, 512, 1)
    rows = value.shape[0]
    split = value.reshape(rows, 4, 4, 128)
    return lax.dynamic_index_in_dim(split, index, 2, keepdims=False).reshape(rows, 512)


def spread_left(left, along, place, shift):
    half = left.shape[0] // 2
    got = []
    for step in SHIFTS:
        mine = shift(model_slice(left[:half], (place + step) % 4, along), step)
        got.append(jnp.concatenate([mine, swap_core(mine)], axis=0))
    return [model_slice(left, place, along)] + got


def finish(total, place, shift, half_x):
    low = total.astype(BF)
    mine = piece(total, place, 128, 0)
    for step in SHIFTS:
        mine = mine + shift(piece(low, (place + step) % 4, 128, 0), step).astype(F32)
    other = piece(mine, 1 - half_x, 64, 0).astype(BF)
    return piece(mine, half_x, 64, 0) + swap_xh(other).astype(F32)


def local(
    tokens,
    segment_ids,
    norm1_gain,
    norm1_shift,
    w_query,
    w_key,
    w_value,
    w_gate,
    w_output,
    norm2_gain,
    norm2_shift,
    w_up,
    w_down,
    cotangent,
):
    tensor = lax.axis_index("tensor")
    dp = lax.axis_index("dp")
    y, z, xh = dp // 8, dp // 2 % 4, dp % 2
    inputs = tokens.astype(F32)
    normed1, factor1 = norm_rows(inputs, 1e-05)
    hidden1_rows = (normed1 * norm1_gain + norm1_shift).astype(BF)
    hidden1 = gather_row(hidden1_rows)
    cot_full = gather_row(cotangent)

    blocks = [tensor, tensor ^ 2, tensor ^ 1, tensor ^ 3]
    position = jnp.concatenate([b * 128 + jnp.arange(128, dtype=jnp.int32) for b in blocks])
    segment = jnp.concatenate([piece(segment_ids, b, 128, 0) for b in blocks])
    half = DK // 2
    freqs = 10000.0 ** (-jnp.arange(half, dtype=F32) / half)
    angle = position.astype(F32)[:, None] * freqs[None, :]
    cosine, sine = jnp.cos(angle), jnp.sin(angle)
    distance = position[:, None] - position[None, :]
    allowed = (segment[:, None] == segment[None, :]) & (distance >= 0)
    steps_back = jnp.where(allowed, distance, 0).astype(F32)

    hidden1_all = [hidden1]
    for step in SHIFTS:
        mine = shift_y(hidden1[:256], step)
        hidden1_all.append(jnp.concatenate([mine, swap_core(mine)], axis=0))

    query_pre = dot(hidden1, w_query)
    key_pre = dot(hidden1, w_key)
    value_low = dot(hidden1, w_value).astype(BF)
    gate_pre = dot(hidden1, w_gate)
    heads = []
    gated_parts = []
    for h in range(2):
        rate = jnp.log(1.0 - 2.0 ** (-5.0 - (tensor * 2 + h).astype(F32)))
        decay = jnp.where(allowed, jnp.exp(steps_back * rate), 0.0) * DK ** (-0.5)
        keys = slice(h * DK, (h + 1) * DK)
        vals = slice(h * DV, (h + 1) * DV)
        query = rotate(query_pre[:, keys], cosine, sine).astype(BF)
        key = rotate(key_pre[:, keys], cosine, sine).astype(BF)
        value = value_low[:, vals]
        scores = (dot_nt(query, key) * decay).astype(BF)
        mixed = dot(scores, value)
        group, group_factor = norm_rows(mixed, 1.0)
        gate = gate_pre[:, vals]
        sigmoid = jax.nn.sigmoid(gate)
        silu = gate * sigmoid
        gated_parts.append((silu * group).astype(BF))
        heads.append((decay, query, key, value, scores, group, group_factor, gate, sigmoid, silu))
    gated = jnp.concatenate(gated_parts, axis=1)

    mid_rows = inputs + scatter_row(dot(gated, w_output), BF)
    normed2, factor2 = norm_rows(mid_rows, 1e-05)
    hidden2_rows = (normed2 * norm2_gain + norm2_shift).astype(BF)
    hidden2 = gather_row(hidden2_rows)

    d_act = dot_nt(cot_full, w_down)
    up_pre = dot(hidden2, w_up)
    tangent = jnp.tanh(0.7978845608 * (up_pre + 0.044715 * up_pre * up_pre * up_pre))
    activated = (0.5 * up_pre * (1.0 + tangent)).astype(BF)
    slope = 0.5 * (1.0 + tangent) + 0.5 * up_pre * (1.0 - tangent * tangent) * 0.7978845608 * (
        1.0 + 3.0 * 0.044715 * up_pre * up_pre
    )
    d_up = (d_act * slope).astype(BF)
    d_hidden2 = scatter_row(dot_nt(d_up, w_up), BF)
    gain2_part = jnp.sum(d_hidden2 * normed2, axis=0)
    shift2_part = jnp.sum(d_hidden2, axis=0)
    d_mid = cotangent.astype(F32) + norm_back(d_hidden2 * norm2_gain, normed2, factor2)
    d_mid_full = gather_row(d_mid.astype(BF))

    block_out = (mid_rows + scatter_row(dot(activated, w_down), BF)).astype(BF)

    cot_slices = spread_left(cot_full, "z", z, shift_z)
    act_all = [activated] + [shift_z(activated, step) for step in SHIFTS]
    down_sum = finish(
        sum(dot_tn(a, b) for a, b in zip(cot_slices, act_all)), y, shift_y, xh
    ).T

    gated_all = [gated] + [shift_y(gated, step) for step in SHIFTS]
    d_up_all = [d_up] + [shift_y(d_up, step) for step in SHIFTS]
    hidden2_slices = spread_left(hidden2, "y", y, shift_y)
    up_sum = finish(
        sum(dot_tn(a, b) for a, b in zip(hidden2_slices, d_up_all)), z, shift_z, xh
    )
    d_mid_slices = spread_left(d_mid_full, "y", y, shift_y)
    output_sum = finish(
        sum(dot_tn(a, b) for a, b in zip(d_mid_slices, gated_all)), z, shift_z, xh
    ).T

    d_gated = dot_nt(d_mid_full, w_output)
    d_query, d_key, d_value, d_gate = [], [], [], []
    for h in range(2):
        decay, query, key, value, scores, group, group_factor, gate, sigmoid, silu = heads[h]
        grad = d_gated[:, h * DV : (h + 1) * DV]
        d_gate.append((grad * group * (sigmoid + silu * (1.0 - sigmoid))).astype(BF))
        d_mixed = norm_back(grad * silu, group, group_factor).astype(BF)
        d_raw = (dot_nt(d_mixed, value) * decay).astype(BF)
        d_query.append(rotate(dot(d_raw, key), cosine, -sine).astype(BF))
        d_key.append(rotate(dot_tn(d_raw, query), cosine, -sine).astype(BF))
        d_value.append(dot_tn(scores, d_mixed).astype(BF))
    d_query, d_key, d_value, d_gate = (
        jnp.concatenate(parts, axis=1) for parts in (d_query, d_key, d_value, d_gate)
    )
    total = (
        dot_nt(d_query, w_query)
        + dot_nt(d_key, w_key)
        + dot_nt(d_value, w_value)
        + dot_nt(d_gate, w_gate)
    )
    d_hidden1 = scatter_row(total, BF)
    gain1_part = jnp.sum(d_hidden1 * normed1, axis=0)
    shift1_part = jnp.sum(d_hidden1, axis=0)
    tokens_grad = d_mid + norm_back(d_hidden1 * norm1_gain, normed1, factor1)

    sums = []
    for grads in ((d_gate,), (d_value,), (d_query, d_key)):
        def columns(index):
            return jnp.concatenate([piece(g, index, g.shape[1] // 4, 1) for g in grads], axis=1)

        rights = [columns(y)] + [shift_y(columns((y + step) % 4), step) for step in SHIFTS]
        part = sum(dot_tn(a, b) for a, b in zip(hidden1_all, rights))
        part = part.reshape(4, 4, 128, 256)
        low = part.astype(BF)
        mine = lax.dynamic_index_in_dim(part, z, 1, keepdims=False)
        for step in SHIFTS:
            sent = lax.dynamic_index_in_dim(low, (z + step) % 4, 1, keepdims=False)
            mine = mine + shift_z(sent, step).astype(F32)
        mine = mine.reshape(4, 2, 64, 256)
        other = lax.dynamic_index_in_dim(mine, 1 - xh, 1, keepdims=False).astype(BF)
        mine = lax.dynamic_index_in_dim(mine, xh, 1, keepdims=False) + swap_xh(other).astype(F32)
        ready = mine.astype(BF)
        result = jnp.zeros((4, 64, 256), F32)
        result = lax.dynamic_update_index_in_dim(
            result, lax.dynamic_index_in_dim(mine, y, 0, keepdims=False), y, 0
        )
        for step in SHIFTS:
            sent = lax.dynamic_index_in_dim(ready, (y + step) % 4, 0, keepdims=False)
            got = shift_y(sent, step).astype(F32)
            result = lax.dynamic_update_index_in_dim(result, got, (y - step) % 4, 0)
        start = 0
        for g in grads:
            width = g.shape[1] // 4
            part = result[:, :, start : start + width]
            sums.append(jnp.transpose(part, (1, 0, 2)).reshape(64, 4 * width))
            start += width
    gate_sum, value_sum, query_sum, key_sum = sums

    stacked = jnp.stack([gain1_part, shift1_part, gain2_part, shift2_part], axis=0)
    spread = stacked.reshape(4, 128, 16).transpose(1, 0, 2).reshape(128, 64)
    spread = lax.all_to_all(spread, ("dp", "tensor"), 0, 0, tiled=True)
    norm_sums = jnp.sum(spread, axis=0).reshape(4, 16)
    return (
        block_out,
        tokens_grad,
        norm_sums[0],
        norm_sums[1],
        query_sum,
        key_sum,
        value_sum,
        gate_sum,
        output_sum,
        norm_sums[2],
        norm_sums[3],
        up_sum,
        down_sum,
    )


def solution(mesh):
    in_specs = (
        P(("dp", "tensor"), None),
        P("dp"),
        P(),
        P(),
        P(None, "tensor"),
        P(None, "tensor"),
        P(None, "tensor"),
        P(None, "tensor"),
        P("tensor", None),
        P(),
        P(),
        P(None, "tensor"),
        P("tensor", None),
        P(("dp", "tensor"), None),
    )
    out_specs = (
        P(("dp", "tensor"), None),
        P(("dp", "tensor"), None),
        P(("dp", "tensor")),
        P(("dp", "tensor")),
        P("dp", "tensor"),
        P("dp", "tensor"),
        P("dp", "tensor"),
        P("dp", "tensor"),
        P("tensor", "dp"),
        P(("dp", "tensor")),
        P(("dp", "tensor")),
        P("dp", "tensor"),
        P("tensor", "dp"),
    )
    return jax.shard_map(local, mesh=mesh, in_specs=in_specs, out_specs=out_specs, check_vma=False)
```

```python
import jax
import jax.numpy as jnp
from jax import lax
from jax.experimental import pallas as pl
from jax.experimental.pallas import tpu as pltpu
from jax.sharding import PartitionSpec as P

DK = 256
DV = 512
F32 = jnp.float32
BF = jnp.bfloat16
LIMIT = 52 * 1024 * 1024


def dot(left, right):
    return jnp.dot(left, right, preferred_element_type=F32)


def dot_tn(left, right):
    return lax.dot_general(left, right, (((0,), (0,)), ((), ())), preferred_element_type=F32)


def dot_nt(left, right):
    return lax.dot_general(left, right, (((1,), (1,)), ((), ())), preferred_element_type=F32)


def norm_rows(value, epsilon):
    centred = value - jnp.mean(value, axis=-1, keepdims=True)
    factor = lax.rsqrt(jnp.mean(centred * centred, axis=-1, keepdims=True) + epsilon)
    return (centred * factor, factor)


def norm_back(grad, normed, factor):
    return factor * (
        grad
        - jnp.mean(grad, axis=-1, keepdims=True)
        - normed * jnp.mean(grad * normed, axis=-1, keepdims=True)
    )


def rotate(value, cosine, sine):
    half = DK // 2
    first = value[:, :half]
    second = value[:, half:]
    return jnp.concatenate(
        [first * cosine - second * sine, first * sine + second * cosine], axis=-1
    )


def decay_of(rate, row_pos, col_pos, row_seg, col_seg):
    distance = row_pos - col_pos
    allowed = (row_seg == col_seg) & (distance >= 0)
    steps_back = jnp.where(allowed, distance, 0).astype(F32)
    return jnp.where(allowed, jnp.exp(steps_back * rate), 0.0) * DK ** (-0.5)


def forward_kernel(
    rates, t0, t1, t2, t3, gain, shift, wq, wk, wv, wg, cosine, sine, prow, pcol, srow, scol,
    h1, q, k, v, gate, group, factor, scores, gated,
):
    head = pl.program_id(0)

    @pl.when(head == 0)
    def _():
        for i, piece in enumerate((t0, t1, t2, t3)):
            normed, _ = norm_rows(piece[...].astype(F32), 1e-05)
            h1[pl.ds(i * 128, 128), :] = (normed * gain[...] + shift[...]).astype(BF)

    hidden = h1[...]
    cos, sin = cosine[...], sine[...]
    q[...] = rotate(dot(hidden, wq[...]), cos, sin).astype(BF)
    k[...] = rotate(dot(hidden, wk[...]), cos, sin).astype(BF)
    v[...] = dot(hidden, wv[...]).astype(BF)
    gate[...] = dot(hidden, wg[...])
    rate = rates[head]
    for i in range(4):
        rows = pl.ds(i * 128, 128)
        decay = decay_of(rate, prow[rows, :], pcol[...], srow[rows, :], scol[...])
        score = (dot_nt(q[rows, :], k[...]) * decay).astype(BF)
        scores[0, rows, :] = score
        normed, spread = norm_rows(dot(score, v[...]), 1.0)
        group[rows, :] = normed
        factor[rows, :] = jnp.broadcast_to(spread, (128, 128))
        g = gate[rows, :]
        gated[rows, :] = (g * jax.nn.sigmoid(g) * normed).astype(BF)


def forward_call(rates, pieces, gain, shift, wq, wk, wv, wg, cosine, sine, pos, seg):
    whole = lambda *shape: pl.BlockSpec(shape, lambda h: (0,) * len(shape))
    cols = lambda rows, n: pl.BlockSpec((rows, n), lambda h: (0, h))
    sd = jax.ShapeDtypeStruct
    return pl.pallas_call(
        forward_kernel,
        grid=(2,),
        in_specs=[pl.BlockSpec(memory_space=pltpu.SMEM)]
        + [whole(128, 2048)] * 4
        + [whole(1, 2048)] * 2
        + [cols(2048, 256)] * 2
        + [cols(2048, 512)] * 2
        + [whole(512, 128)] * 2
        + [whole(512, 1), whole(1, 512)] * 2,
        out_specs=[
            whole(512, 2048), cols(512, 256), cols(512, 256), cols(512, 512), cols(512, 512),
            cols(512, 512), cols(512, 128),
            pl.BlockSpec((1, 512, 512), lambda h: (h, 0, 0)), cols(512, 512),
        ],
        out_shape=[
            sd((512, 2048), BF), sd((512, 512), BF), sd((512, 512), BF), sd((512, 1024), BF),
            sd((512, 1024), F32), sd((512, 1024), F32), sd((512, 256), F32),
            sd((2, 512, 512), BF), sd((512, 1024), BF),
        ],
        compiler_params=pltpu.CompilerParams(vmem_limit_bytes=LIMIT),
        cost_estimate=pl.CostEstimate(flops=8_000_000_000, bytes_accessed=24_000_000, transcendentals=0),
        name="retention_forward",
    )(rates, *pieces, gain[None], shift[None], wq, wk, wv, wg, cosine, sine,
      pos[:, None], pos[None], seg[:, None], seg[None])


def backward_kernel(
    rates, d0, d1, d2, d3, wo, cosine, sine, prow, pcol, srow, scol,
    q, k, v, gate, group, factor, scores, dq, dk, dv, dg, grad, mixed, raw,
):
    head = pl.program_id(0)
    for i, piece in enumerate((d0, d1, d2, d3)):
        grad[pl.ds(i * 128, 128), :] = dot_nt(piece[...], wo[...])
    rate = rates[head]
    for i in range(4):
        rows = pl.ds(i * 128, 128)
        g, d, gn = gate[rows, :], grad[rows, :], group[rows, :]
        sig = jax.nn.sigmoid(g)
        silu = g * sig
        dg[rows, :] = (d * gn * (sig + silu * (1.0 - sig))).astype(BF)
        dm = norm_back(d * silu, gn, factor[rows, :1]).astype(BF)
        mixed[rows, :] = dm
        decay = decay_of(rate, prow[rows, :], pcol[...], srow[rows, :], scol[...])
        dr = (dot_nt(dm, v[...]) * decay).astype(BF)
        raw[rows, :] = dr
        dq[rows, :] = rotate(dot(dr, k[...]), cosine[rows, :], -sine[rows, :]).astype(BF)
    dv[...] = dot_tn(scores[0], mixed[...]).astype(BF)
    dk[...] = rotate(dot_tn(raw[...], q[...]), cosine[...], -sine[...]).astype(BF)


def backward_call(rates, pieces, wo, cosine, sine, pos, seg, saved):
    whole = lambda *shape: pl.BlockSpec(shape, lambda h: (0,) * len(shape))
    cols = lambda rows, n: pl.BlockSpec((rows, n), lambda h: (0, h))
    sd = jax.ShapeDtypeStruct
    return pl.pallas_call(
        backward_kernel,
        grid=(2,),
        in_specs=[pl.BlockSpec(memory_space=pltpu.SMEM)]
        + [whole(128, 2048)] * 4
        + [pl.BlockSpec((512, 2048), lambda h: (h, 0))]
        + [whole(512, 128)] * 2
        + [whole(512, 1), whole(1, 512)] * 2
        + [cols(512, 256), cols(512, 256), cols(512, 512), cols(512, 512), cols(512, 512),
           cols(512, 128), pl.BlockSpec((1, 512, 512), lambda h: (h, 0, 0))],
        out_specs=[cols(512, 256), cols(512, 256), cols(512, 512), cols(512, 512)],
        out_shape=[sd((512, 512), BF), sd((512, 512), BF), sd((512, 1024), BF), sd((512, 1024), BF)],
        scratch_shapes=[
            pltpu.VMEM((512, 512), F32), pltpu.VMEM((512, 512), BF), pltpu.VMEM((512, 512), BF),
        ],
        compiler_params=pltpu.CompilerParams(vmem_limit_bytes=LIMIT),
        cost_estimate=pl.CostEstimate(flops=5_000_000_000, bytes_accessed=18_000_000, transcendentals=0),
        name="retention_backward",
    )(rates, *pieces, wo, cosine, sine, pos[:, None], pos[None], seg[:, None], seg[None], *saved)


def middle_kernel(tokens, near, far, gain, shift, x2, h2):
    mid = tokens[...].astype(F32) + near[...] + far[...].astype(F32)
    x2[...] = mid
    normed, _ = norm_rows(mid, 1e-05)
    h2[...] = (normed * gain[...] + shift[...]).astype(BF)


def middle_call(tokens, near, far, gain, shift):
    sd = jax.ShapeDtypeStruct
    return pl.pallas_call(
        middle_kernel,
        out_shape=[sd((128, 2048), F32), sd((128, 2048), BF)],
        compiler_params=pltpu.CompilerParams(vmem_limit_bytes=LIMIT),
        cost_estimate=pl.CostEstimate(flops=4_000_000, bytes_accessed=4_000_000, transcendentals=0),
        name="second_norm",
    )(tokens, near, far, gain[None], shift[None])


def norm_back_kernel(near, far, rows, gain, outer, grad, low, sums):
    d = near[...] + far[...].astype(F32)
    normed, factor = norm_rows(rows[...].astype(F32), 1e-05)
    sums[0:1, :] = jnp.sum(d * normed, axis=0, keepdims=True)
    sums[1:2, :] = jnp.sum(d, axis=0, keepdims=True)
    total = outer[...].astype(F32) + norm_back(d * gain[...], normed, factor)
    grad[...] = total
    low[...] = total.astype(BF)


def norm_back_call(near, far, rows, gain, outer, name):
    sd = jax.ShapeDtypeStruct
    return pl.pallas_call(
        norm_back_kernel,
        out_shape=[sd((128, 2048), F32), sd((128, 2048), BF), sd((2, 2048), F32)],
        compiler_params=pltpu.CompilerParams(vmem_limit_bytes=LIMIT),
        cost_estimate=pl.CostEstimate(flops=8_000_000, bytes_accessed=5_000_000, transcendentals=0),
        name=name,
    )(near, far, rows, gain[None], outer)


def feed_forward_kernel(
    h0, h1, h2, h3, w_up, d_act, act, d_up, p0, p1, p2, p3, total
):
    step = pl.program_id(0)
    pieces = (h0, h1, h2, h3)
    outs = (p0, p1, p2, p3)
    weights = w_up[...]
    for i in range(4):
        rows = pl.ds(i * 128, 128)
        u = dot(pieces[i][...], weights)
        square = u * u
        t = jnp.tanh(0.7978845608 * (u + 0.044715 * u * square))
        act[rows, :] = (0.5 * u * (1.0 + t)).astype(BF)
        slope = 0.5 * (1.0 + t) + 0.5 * u * (1.0 - t * t) * 0.7978845608 * (
            1.0 + 3.0 * 0.044715 * square
        )
        low = (d_act[rows, :] * slope).astype(BF)
        d_up[rows, :] = low
        part = dot_nt(low, weights)

        @pl.when(step == 0)
        def _():
            total[rows, :] = part

        @pl.when(step > 0)
        def _():
            total[rows, :] += part

    @pl.when(step == pl.num_programs(0) - 1)
    def _():
        for i in range(4):
            outs[i][...] = total[pl.ds(i * 128, 128), :].astype(outs[i].dtype)


def feed_forward_call(pieces, w_up, d_act):
    whole = lambda *shape: pl.BlockSpec(shape, lambda f: (0,) * len(shape))
    cols = lambda rows, n: pl.BlockSpec((rows, n), lambda f: (0, f))
    sd = jax.ShapeDtypeStruct
    return pl.pallas_call(
        feed_forward_kernel,
        grid=(4,),
        in_specs=[whole(128, 2048)] * 4 + [cols(2048, 256), cols(512, 256)],
        out_specs=[cols(512, 256)] * 2 + [whole(128, 2048)] * 4,
        out_shape=[sd((512, 1024), BF)] * 2
        + [sd((128, 2048), F32)] * 2
        + [sd((128, 2048), BF)] * 2,
        scratch_shapes=[pltpu.VMEM((512, 2048), F32)],
        compiler_params=pltpu.CompilerParams(vmem_limit_bytes=LIMIT),
        cost_estimate=pl.CostEstimate(flops=5_000_000_000, bytes_accessed=12_000_000, transcendentals=0),
        name="feed_forward",
    )(*pieces, w_up, d_act)


def weight_kernel(x_own, a1, b1, a2, b2, a3, b3, y_own, y1, y2, y3, out, flip):
    @pl.when(pl.program_id(0) == 0)
    def _():
        for i, grad in enumerate((y_own, y1, y2, y3)):
            flip[:, pl.ds(i * 512, 512)] = jnp.transpose(grad[...])

    total = dot(flip[:, :512], x_own[...])
    for i, piece in enumerate((a1, b1, a2, b2, a3, b3)):
        total += dot(flip[:, 512 + i * 256 : 768 + i * 256], piece[...])
    low = total.astype(BF)
    for z in range(4):
        out[z] = low[:, z * 128 : (z + 1) * 128]


def weight_call(lefts, rights):
    cols = rights[0].shape[1]
    sd = jax.ShapeDtypeStruct
    return pl.pallas_call(
        weight_kernel,
        grid=(4,),
        in_specs=[pl.BlockSpec((x.shape[0], 512), lambda y: (0, y)) for x in lefts]
        + [pl.BlockSpec((512, cols), lambda y: (0, 0))] * 4,
        out_specs=pl.BlockSpec((4, cols, 128), lambda y: (0, 0, y)),
        out_shape=sd((4, cols, 512), BF),
        scratch_shapes=[pltpu.VMEM((cols, 2048), BF)],
        compiler_params=pltpu.CompilerParams(vmem_limit_bytes=LIMIT),
        cost_estimate=pl.CostEstimate(flops=8_000_000 * cols, bytes_accessed=12_000_000, transcendentals=0),
        name="projection_weights",
    )(*lefts, *rights)


def sum_kernel(own, r1, r2, r3, out):
    total = own[...].astype(F32) + r1[...].astype(F32)
    total += r2[...].astype(F32) + r3[...].astype(F32)
    out[...] = jnp.transpose(total).astype(BF)


def sum_call(parts):
    cols = parts[0].shape[0]
    return pl.pallas_call(
        sum_kernel,
        out_shape=jax.ShapeDtypeStruct((512, cols), BF),
        compiler_params=pltpu.CompilerParams(vmem_limit_bytes=LIMIT),
        cost_estimate=pl.CostEstimate(flops=4_000_000, bytes_accessed=2_000_000, transcendentals=0),
        name="projection_sum",
    )(*parts)


SHIFTS = (1, -1, 2)


def shift_y(value, step):
    return lax.ppermute(
        value, "dp", [(i, ((i // 8 + step) % 4) * 8 + i % 8) for i in range(32)]
    )


def shift_z(value, step):
    return lax.ppermute(
        value,
        "dp",
        [(i, (i // 8) * 8 + ((i // 2 % 4 + step) % 4) * 2 + i % 2) for i in range(32)],
    )


def swap_xh(value):
    return lax.ppermute(value, "dp", [(i, i ^ 1) for i in range(32)])


def swap_xl(value):
    return lax.ppermute(value, "tensor", [(i, i ^ 2) for i in range(4)])


def swap_core(value):
    return lax.ppermute(value, "tensor", [(i, i ^ 1) for i in range(4)])


GROUPS_Y = [[y * 8 + r for y in range(4)] for r in range(8)]
GROUPS_Z = [[y * 8 + z * 2 + r for z in range(4)] for y in range(4) for r in range(2)]
GROUPS_YX = [[y * 8 + z * 2 + r for y in range(4) for r in range(2)] for z in range(4)]


def after(value, *others):
    return lax.optimization_barrier((value,) + others)[0]


def gather_row(own):
    across = swap_xl(own)
    return [own, across, swap_core(own), swap_core(across)]


def scatter_row(parts, hold=None):
    far = (parts[1] + swap_core(parts[3].astype(BF)).astype(F32)).astype(BF)
    near = parts[0] + swap_core(parts[2].astype(BF)).astype(F32)
    if hold is not None:
        far = after(far, hold)
    return near, swap_xl(far), far


def rows_of(value):
    return [value[i * 128 : (i + 1) * 128] for i in range(4)]


def piece(value, index, size, axis):
    return lax.dynamic_slice_in_dim(value, index * size, size, axis)


def model_slice(value, index, along):
    if along == "y":
        return piece(value, index, 512, 1)
    return jnp.concatenate(
        [lax.dynamic_slice_in_dim(value, y * 512 + index * 128, 128, 1) for y in range(4)], axis=1
    )


def spread_left(half, along, place, shift):
    return [shift(model_slice(half, (place + step) % 4, along), step) for step in SHIFTS]


def both_cores(parts):
    return [jnp.concatenate([p, swap_core(p)], axis=0) for p in parts]


def local(
    tokens,
    segment_ids,
    norm1_gain,
    norm1_shift,
    w_query,
    w_key,
    w_value,
    w_gate,
    w_output,
    norm2_gain,
    norm2_shift,
    w_up,
    w_down,
    cotangent,
):
    tensor = lax.axis_index("tensor")
    dp = lax.axis_index("dp")
    y, z, xh = dp // 8, dp // 2 % 4, dp % 2

    pieces = gather_row(tokens)
    blocks = [tensor, tensor ^ 2, tensor ^ 1, tensor ^ 3]
    pos = jnp.concatenate([b * 128 + jnp.arange(128, dtype=jnp.int32) for b in blocks])
    seg = jnp.concatenate([piece(segment_ids, b, 128, 0) for b in blocks])
    half = DK // 2
    freqs = 10000.0 ** (-jnp.arange(half, dtype=F32) / half)
    angle = pos.astype(F32)[:, None] * freqs[None, :]
    cosine, sine = jnp.cos(angle), jnp.sin(angle)
    heads = (tensor * 2 + jnp.arange(2)).astype(F32)
    rates = jnp.log(1.0 - 2.0 ** (-5.0 - heads))

    hidden1, query, key, value, gate, group, factor, scores, gated = forward_call(
        rates, pieces, norm1_gain, norm1_shift, w_query, w_key, w_value, w_gate, cosine, sine, pos, seg
    )
    cot = gather_row(after(cotangent, pieces[1]))

    near, far, sent = scatter_row(rows_of(dot(gated, w_output)))
    hidden1_half = after(hidden1[:256], sent)
    hidden1_a = [shift_y(hidden1_half, step) for step in SHIFTS]
    gated_sent = after(gated, sent)
    gated_all = [gated] + [shift_z(gated_sent, step) for step in SHIFTS]
    mid_rows, hidden2_rows = middle_call(tokens, near, far, norm2_gain, norm2_shift)

    hidden2 = gather_row(hidden2_rows)
    cot_low = jnp.concatenate(cot, axis=0)
    d_act = dot_nt(cot_low, w_down)
    activated, d_up, p0, p1, p2, p3 = feed_forward_call(hidden2, w_up, d_act)
    near, far, sent = scatter_row([p0, p1, p2, p3])
    act_sent = after(activated, sent)
    act_all = [activated] + [shift_z(act_sent, step) for step in SHIFTS]
    d_up_sent = after(d_up, sent)
    d_up_all = [d_up] + [shift_y(d_up_sent, step) for step in SHIFTS]
    cot_half = after(jnp.concatenate(cot[:2], axis=0), sent)
    cot_parts = spread_left(cot_half, "z", z, shift_z)
    hidden2_half = after(jnp.concatenate(hidden2[:2], axis=0), sent)
    hidden2_parts = spread_left(hidden2_half, "y", y, shift_y)
    d_mid, d_mid_low, sums2 = norm_back_call(
        near, far, mid_rows, norm2_gain, cotangent, "second_norm_back"
    )

    d_mid_pieces = gather_row(d_mid_low)
    d_query, d_key, d_value, d_gate = backward_call(
        rates, d_mid_pieces, w_output, cosine, sine, pos, seg,
        (query, key, value, gate, group, factor, scores),
    )

    def columns(grads, index):
        return jnp.concatenate([piece(g, index, g.shape[1] // 4, 1) for g in grads], axis=1)

    rights = []
    for grads in ((d_gate, d_value), (d_query, d_key)):
        rights.append(
            [columns(grads, y)]
            + [shift_y(columns(grads, (y + step) % 4), step) for step in SHIFTS]
        )
    d_mid_parts = spread_left(jnp.concatenate(d_mid_pieces[:2], axis=0), "z", z, shift_z)

    total = (
        dot_nt(d_query, w_query)
        + dot_nt(d_key, w_key)
        + dot_nt(d_value, w_value)
        + dot_nt(d_gate, w_gate)
    )
    near, far, sent1 = scatter_row(rows_of(total))
    tokens_grad, _, sums1 = norm_back_call(near, far, tokens, norm1_gain, d_mid, "first_norm_back")

    near, far, _ = scatter_row(rows_of(dot(activated, w_down)), d_mid_pieces[1])
    block_out = (mid_rows + near + far.astype(F32)).astype(BF)

    def partial(lefts, rights):
        return sum(dot_tn(a, b) for a, b in zip(lefts, rights)).astype(BF)

    def reduce(part, groups):
        return lax.psum_scatter(
            part, "dp", scatter_dimension=0, axis_index_groups=groups, tiled=True
        )

    cot_slices = [model_slice(cot_low, z, "z")] + both_cores([after(p, d_mid_low) for p in cot_parts])
    down_part = reduce(partial(cot_slices, act_all), GROUPS_Y)
    hidden2_slices = [model_slice(jnp.concatenate(hidden2, axis=0), y, "y")] + both_cores(
        [after(p, d_mid_low) for p in hidden2_parts]
    )
    up_part = reduce(partial(hidden2_slices, d_up_all), GROUPS_Z)
    d_mid_slices = [model_slice(jnp.concatenate(d_mid_pieces, axis=0), z, "z")] + both_cores(
        [after(p, sent1) for p in d_mid_parts]
    )
    output_part = reduce(partial(d_mid_slices, gated_all), GROUPS_Y)
    parts = jnp.stack([down_part, up_part, output_part])
    mine = piece(parts, xh, 64, 1).astype(F32) + swap_xh(piece(parts, 1 - xh, 64, 1)).astype(F32)
    down_sum, up_sum, output_sum = mine[0].T, mine[1], mine[2].T

    hidden1_parts = [after(p, d_mid_low) for p in hidden1_a]
    lefts = [hidden1]
    for p in hidden1_parts:
        lefts += [p, swap_core(p)]
    ready = []
    for right in rights:
        part = weight_call(lefts, right)
        got = [lax.dynamic_index_in_dim(part, z, 0, keepdims=False)]
        for step in SHIFTS:
            sent = lax.dynamic_index_in_dim(part, (z + step) % 4, 0, keepdims=False)
            got.append(shift_z(sent, step))
        ready.append(sum_call(got))
    ready = jnp.concatenate(ready, axis=1).reshape(8, 64, 768)
    got = lax.all_to_all(ready, "dp", 0, 0, axis_index_groups=GROUPS_YX, tiled=True)
    got = got.reshape(4, 2, 64, 768).astype(F32)
    got = got[:, 0] + got[:, 1]
    gate_sum, value_sum, query_sum, key_sum = (
        jnp.concatenate([got[i][:, a:b] for i in range(4)], axis=1)
        for a, b in ((0, 256), (256, 512), (512, 640), (640, 768))
    )

    spread = jnp.concatenate([sums1, sums2], axis=0).reshape(4, 128, 16)
    spread = spread.transpose(1, 0, 2).reshape(128, 64)
    spread = lax.all_to_all(spread, ("dp", "tensor"), 0, 0, tiled=True)
    norm_sums = jnp.sum(spread, axis=0).reshape(4, 16)
    return (
        block_out,
        tokens_grad,
        norm_sums[0],
        norm_sums[1],
        query_sum,
        key_sum,
        value_sum,
        gate_sum,
        output_sum,
        norm_sums[2],
        norm_sums[3],
        up_sum,
        down_sum,
    )


def solution(mesh):
    in_specs = (
        P(("dp", "tensor"), None),
        P("dp"),
        P(),
        P(),
        P(None, "tensor"),
        P(None, "tensor"),
        P(None, "tensor"),
        P(None, "tensor"),
        P("tensor", None),
        P(),
        P(),
        P(None, "tensor"),
        P("tensor", None),
        P(("dp", "tensor"), None),
    )
    out_specs = (
        P(("dp", "tensor"), None),
        P(("dp", "tensor"), None),
        P(("dp", "tensor")),
        P(("dp", "tensor")),
        P("dp", "tensor"),
        P("dp", "tensor"),
        P("dp", "tensor"),
        P("dp", "tensor"),
        P("tensor", "dp"),
        P(("dp", "tensor")),
        P(("dp", "tensor")),
        P("dp", "tensor"),
        P("tensor", "dp"),
    )
    return jax.shard_map(local, mesh=mesh, in_specs=in_specs, out_specs=out_specs, check_vma=False)
```

```python
import functools

import jax
import jax.numpy as jnp
import numpy as np
from jax import lax
from jax.experimental import pallas as pl
from jax.experimental.pallas import tpu as pltpu
from jax.sharding import PartitionSpec as P

DK = 256
DV = 512
F32 = jnp.float32
BF = jnp.bfloat16
SHIFTS = (1, -1, 2)


def dot(left, right):
    return jnp.dot(left, right, preferred_element_type=F32)


def dot_tn(left, right):
    return lax.dot_general(left, right, (((0,), (0,)), ((), ())), preferred_element_type=F32)


def dot_nt(left, right):
    return lax.dot_general(left, right, (((1,), (1,)), ((), ())), preferred_element_type=F32)


def norm_rows(value, epsilon):
    centred = value - jnp.mean(value, axis=-1, keepdims=True)
    factor = lax.rsqrt(jnp.mean(centred * centred, axis=-1, keepdims=True) + epsilon)
    return (centred * factor, factor)


def norm_back(grad, normed, factor):
    return factor * (
        grad
        - jnp.mean(grad, axis=-1, keepdims=True)
        - normed * jnp.mean(grad * normed, axis=-1, keepdims=True)
    )


def rotate(value, cosine, sine):
    half = DK // 2
    first = value[:, :half]
    second = value[:, half:]
    return jnp.concatenate(
        [first * cosine - second * sine, first * sine + second * cosine], axis=-1
    )


def rotation_table():
    half = DK // 2
    freqs = 10000.0 ** (-np.arange(half, dtype=np.float64) / half)
    angle = np.arange(512, dtype=np.float64)[:, None] * freqs[None, :]
    return np.concatenate([np.cos(angle), np.sin(angle)], axis=1).astype(np.float32)


def device_info(y, z, tensor):
    k = np.zeros((6, 32), np.int32)
    k[0, PLACES : PLACES + 4] = (0, 2, 1, 3)
    k[4, PLACES : PLACES + 4] = 1
    k[1, REL_Y : REL_Y + 4], k[3, REL_Y : REL_Y + 4], k[4, REL_Y : REL_Y + 4] = -1, range(4), 2
    for start, factor in ((ORDER_Y, 1), (ORDER_Z, 2)):
        k[factor, start : start + 4] = 1
        k[3, start : start + 4] = (0, 1, 3, 2)
        k[4, start : start + 4] = 3
    for start, factor in ((SOURCE_Y, 1), (SOURCE_Z, 2)):
        k[factor, start : start + 4] = 1
        k[3, start : start + 4] = (0, 3, 1, 2)
        k[4, start : start + 4] = 3
    added = (k[1] * y + k[2] * z + k[3]) & 3
    return jnp.where(
        k[4] == 1,
        tensor ^ k[0],
        jnp.where(k[4] == 2, added ^ (added >> 1), jnp.where(k[4] == 3, added, tensor * 2)),
    ).astype(jnp.int32)


PLACES, REL_Y, ORDER_Y, SOURCE_Y, ORDER_Z, SOURCE_Z, HEAD = 0, 4, 8, 12, 16, 20, 24
RATES = np.log1p(-(2.0 ** (-5.0 - np.arange(8)))).astype(np.float32)


def params(megabytes):
    return pltpu.CompilerParams(vmem_limit_bytes=megabytes * 1024 * 1024)


def lasts(microseconds):
    return pl.CostEstimate(
        flops=int(microseconds * 0.3e9), bytes_accessed=100_000, transcendentals=0
    )


def whole(*shape):
    return pl.BlockSpec(shape, lambda i: (0,) * len(shape))


def cols(rows, n):
    return pl.BlockSpec((rows, n), lambda i: (0, i))


def scalars():
    return pl.BlockSpec(memory_space=pltpu.SMEM)


def like(shape, dtype):
    return jax.ShapeDtypeStruct(shape, dtype)


def decay_of(block, rate, info, seg_row, seg_t):
    rows = info[PLACES + block] * 128 + lax.broadcasted_iota(jnp.int32, (128, 512), 0)
    inner = lax.broadcasted_iota(jnp.int32, (1, 128), 1)
    columns = jnp.concatenate([info[PLACES + i] * 128 + inner for i in range(4)], axis=1)
    distance = rows - columns
    allowed = (seg_t[pl.ds(block * 128, 128), :1] == seg_row[...]) & (distance >= 0)
    steps_back = jnp.where(allowed, distance, 0).astype(F32)
    return jnp.where(allowed, jnp.exp(steps_back * rate), 0.0) * DK ** (-0.5)


def turn_of(block, info, table):
    rows = table[pl.ds(pl.multiple_of(info[PLACES + block] * 128, 128), 128), :]
    return rows[:, : DK // 2], rows[:, DK // 2 :]


def flip_row(info, seg, seg_row, seg_t):
    held = jnp.concatenate([seg[pl.ds(info[PLACES + i], 1), :] for i in range(4)], axis=1)
    held = held.astype(F32)
    seg_row[...] = held
    seg_t[...] = jnp.transpose(jnp.broadcast_to(held, (128, 512)))


def forward_kernel(
    info, rates, t0, t1, t2, t3, gain, shift, wq, wk, wv, wg, table, seg,
    h1, q, k, v, gate, group, factor, scores, gated, seg_row, seg_t, pre,
):
    head = pl.program_id(0)

    @pl.when(head == 0)
    def _():
        flip_row(info, seg, seg_row, seg_t)
        for i, piece in enumerate((t0, t1, t2, t3)):
            normed, _ = norm_rows(piece[...].astype(F32), 1e-05)
            h1[pl.ds(i * 128, 128), :] = (normed * gain[...] + shift[...]).astype(BF)

    hidden = h1[...]
    for weights, out in ((wq, q), (wk, k)):
        pre[...] = dot(hidden, weights[...])
        for i in range(4):
            rows = pl.ds(i * 128, 128)
            out[rows, :] = rotate(pre[rows, :], *turn_of(i, info, table)).astype(BF)
    v[...] = dot(hidden, wv[...]).astype(BF)
    gate[...] = dot(hidden, wg[...])
    for i in range(4):
        rows = pl.ds(i * 128, 128)
        decay = decay_of(i, rates[info[HEAD] + head], info, seg_row, seg_t)
        score = (dot_nt(q[rows, :], k[...]) * decay).astype(BF)
        scores[0, rows, :] = score
        normed, spread = norm_rows(dot(score, v[...]), 1.0)
        group[rows, :] = normed
        factor[rows, :] = jnp.broadcast_to(spread, (128, 128))
        g = gate[rows, :]
        gated[rows, :] = (g * jax.nn.sigmoid(g) * normed).astype(BF)


def forward_call(info, pieces, gain, shift, wq, wk, wv, wg, table, seg):
    return pl.pallas_call(
        forward_kernel,
        grid=(2,),
        in_specs=[scalars()] * 2
        + [whole(128, 2048)] * 4
        + [whole(1, 2048)] * 2
        + [cols(2048, 256)] * 2
        + [cols(2048, 512)] * 2
        + [whole(512, 256), whole(4, 128)],
        out_specs=[
            whole(512, 2048), cols(512, 256), cols(512, 256), cols(512, 512), cols(512, 512),
            cols(512, 512), cols(512, 128),
            pl.BlockSpec((1, 512, 512), lambda h: (h, 0, 0)), cols(512, 512),
        ],
        out_shape=[
            like((512, 2048), BF), like((512, 512), BF), like((512, 512), BF),
            like((512, 1024), BF), like((512, 1024), F32), like((512, 1024), F32),
            like((512, 256), F32), like((2, 512, 512), BF), like((512, 1024), BF),
        ],
        scratch_shapes=[
            pltpu.VMEM((1, 512), F32), pltpu.VMEM((512, 128), F32), pltpu.VMEM((512, 256), F32),
        ],
        compiler_params=params(62),
        cost_estimate=lasts(17),
        name="retention_forward",
    )(info, RATES, *pieces, gain[None], shift[None], wq, wk, wv, wg, table, seg)


def backward_kernel(
    info, rates, d0, d1, d2, d3, wo, table, seg, q, k, v, gate, group, factor, scores,
    dq, dk, dv, dg, gv0, gv1, gv2, gv3, qk0, qk1, qk2, qk3, flipped, seg_row, seg_t, full, grad, mixed, raw, pre,
):
    head = pl.program_id(0)

    @pl.when(head == 0)
    def _():
        flip_row(info, seg, seg_row, seg_t)
        for i, piece in enumerate((d0, d1, d2, d3)):
            full[pl.ds(i * 128, 128), :] = piece[...]
        for i, piece in enumerate((d0, d1)):
            for y in range(4):
                for z in range(4):
                    block = piece[:, y * 512 + z * 128 : y * 512 + z * 128 + 128]
                    flipped[z, y * 128 : y * 128 + 128, i * 128 : i * 128 + 128] = jnp.transpose(block)

    grad[...] = dot_nt(full[...], wo[...])
    for i in range(4):
        rows = pl.ds(i * 128, 128)
        g, d, gn = gate[rows, :], grad[rows, :], group[rows, :]
        sig = jax.nn.sigmoid(g)
        silu = g * sig
        dg[rows, :] = (d * gn * (sig + silu * (1.0 - sig))).astype(BF)
        dm = norm_back(d * silu, gn, factor[rows, :1]).astype(BF)
        mixed[rows, :] = dm
        decay = decay_of(i, rates[info[HEAD] + head], info, seg_row, seg_t)
        dr = (dot_nt(dm, v[...]) * decay).astype(BF)
        raw[rows, :] = dr
        cosine, sine = turn_of(i, info, table)
        dq[rows, :] = rotate(dot(dr, k[...]), cosine, -sine).astype(BF)
    dv[...] = dot_tn(scores[0], mixed[...]).astype(BF)
    pre[...] = dot_tn(raw[...], q[...])
    for i in range(4):
        rows = pl.ds(i * 128, 128)
        cosine, sine = turn_of(i, info, table)
        dk[rows, :] = rotate(pre[rows, :], cosine, -sine).astype(BF)
    for i in range(2):
        target = info[REL_Y + head * 2 + i]
        for s, (gv, qk) in enumerate(((gv0, qk0), (gv1, qk1), (gv2, qk2), (gv3, qk3))):

            @pl.when(target == s)
            def _():
                gv[:, :256] = dg[:, i * 256 : (i + 1) * 256]
                gv[:, 256:] = dv[:, i * 256 : (i + 1) * 256]
                qk[:, :128] = dq[:, i * 128 : (i + 1) * 128]
                qk[:, 128:] = dk[:, i * 128 : (i + 1) * 128]


def backward_call(info, pieces, wo, table, seg, saved):
    return pl.pallas_call(
        backward_kernel,
        grid=(2,),
        in_specs=[scalars()] * 2
        + [whole(128, 2048)] * 4
        + [pl.BlockSpec((512, 2048), lambda h: (h, 0))]
        + [whole(512, 256), whole(4, 128)]
        + [cols(512, 256), cols(512, 256), cols(512, 512), cols(512, 512), cols(512, 512),
           cols(512, 128), pl.BlockSpec((1, 512, 512), lambda h: (h, 0, 0))],
        out_specs=[cols(512, 256), cols(512, 256), cols(512, 512), cols(512, 512)]
        + [whole(512, 512)] * 4
        + [whole(512, 256)] * 4
        + [whole(4, 512, 256)],
        out_shape=[like((512, 512), BF)] * 2
        + [like((512, 1024), BF)] * 2
        + [like((512, 512), BF)] * 4
        + [like((512, 256), BF)] * 4
        + [like((4, 512, 256), BF)],
        scratch_shapes=[
            pltpu.VMEM((1, 512), F32), pltpu.VMEM((512, 128), F32), pltpu.VMEM((512, 2048), BF),
            pltpu.VMEM((512, 512), F32), pltpu.VMEM((512, 512), BF), pltpu.VMEM((512, 512), BF),
            pltpu.VMEM((512, 256), F32),
        ],
        compiler_params=params(62),
        cost_estimate=lasts(1),
        name="retention_backward",
    )(info, RATES, *pieces, wo, table, seg, *saved)


def middle_kernel(tokens, near, side, far, gain, shift, x2, h2):
    mid = tokens[...].astype(F32) + (near[...].astype(F32) + side[...].astype(F32))
    mid += far[...].astype(F32)
    x2[...] = mid
    normed, _ = norm_rows(mid, 1e-05)
    h2[...] = (normed * gain[...] + shift[...]).astype(BF)


def middle_call(tokens, row, gain, shift):
    return pl.pallas_call(
        middle_kernel,
        out_shape=[like((128, 2048), F32), like((128, 2048), BF)],
        compiler_params=params(62),
        cost_estimate=lasts(3),
        name="second_norm",
    )(tokens, *row, gain[None], shift[None])


def norm_back_kernel(near, side, far, rows, gain, outer, grad, low, sums):
    d = near[...].astype(F32) + side[...].astype(F32) + far[...].astype(F32)
    normed, factor = norm_rows(rows[...].astype(F32), 1e-05)
    sums[0:1, :] = jnp.sum(d * normed, axis=0, keepdims=True)
    sums[1:2, :] = jnp.sum(d, axis=0, keepdims=True)
    total = outer[...].astype(F32) + norm_back(d * gain[...], normed, factor)
    grad[...] = total
    low[...] = total.astype(BF)


def norm_back_call(row, rows, gain, outer, name):
    return pl.pallas_call(
        norm_back_kernel,
        out_shape=[like((128, 2048), F32), like((128, 2048), BF), like((2, 2048), F32)],
        compiler_params=params(62),
        cost_estimate=lasts(1),
        name=name,
    )(*row, rows, gain[None], outer)


def add_kernel(left, right, out):
    out[...] = (left[...].astype(F32) + right[...].astype(F32)).astype(BF)


def add_call(left, right):
    return pl.pallas_call(
        add_kernel,
        out_shape=like((128, 2048), BF),
        compiler_params=params(62),
        cost_estimate=lasts(2),
        name="chip_sum",
    )(left, right)


def flip_kernel(first, second, out):
    out[:, :128] = jnp.transpose(first[...])
    out[:, 128:] = jnp.transpose(second[...])


def flip_call(first, second):
    return pl.pallas_call(
        flip_kernel,
        grid=(4,),
        in_specs=[cols(128, 512)] * 2,
        out_specs=pl.BlockSpec((512, 256), lambda i: (i, 0)),
        out_shape=like((2048, 256), BF),
        compiler_params=params(62),
        cost_estimate=lasts(3.6),
        name="flip_tokens",
    )(first, second)


def feed_forward_kernel(
    h0, h1, h2, h3, w_up, d_act, act, d_up, full, p0, p1, p2, p3, total, pre,
):
    step = pl.program_id(0)

    @pl.when(step == 0)
    def _():
        for i, piece in enumerate((h0, h1, h2, h3)):
            full[pl.ds(i * 128, 128), :] = piece[...]

    pre[...] = dot(full[...], w_up[...])
    for i in range(4):
        rows = pl.ds(i * 128, 128)
        u = pre[rows, :]
        square = u * u
        t = jnp.tanh(0.7978845608 * (u + 0.044715 * u * square))
        act[rows, :] = (0.5 * u * (1.0 + t)).astype(BF)
        slope = 0.5 * (1.0 + t) + 0.5 * u * (1.0 - t * t) * 0.7978845608 * (
            1.0 + 3.0 * 0.044715 * square
        )
        d_up[rows, :] = (d_act[rows, :] * slope).astype(BF)

    outs = (p0, p1, p2, p3)

    @pl.when(step == 0)
    def _():
        total[...] = dot_nt(d_up[...], w_up[...])

    @pl.when(step == 1)
    def _():
        for i in range(4):
            columns = pl.ds(i * 512, 512)
            part = dot_nt(d_up[...], w_up[columns, :])
            for j in range(4):
                rows = pl.ds(j * 128, 128)
                value = part[j * 128 : (j + 1) * 128] + total[rows, columns]
                outs[j][:, columns] = value.astype(BF)


def feed_forward_call(pieces, w_up, d_act):
    return pl.pallas_call(
        feed_forward_kernel,
        grid=(2,),
        in_specs=[whole(128, 2048)] * 4 + [cols(2048, 512), cols(512, 512)],
        out_specs=[cols(512, 512)] * 2
        + [whole(512, 2048)]
        + [whole(128, 2048)] * 4,
        out_shape=[like((512, 1024), BF)] * 2
        + [like((512, 2048), BF)]
        + [like((128, 2048), BF)] * 4,
        scratch_shapes=[pltpu.VMEM((512, 2048), F32), pltpu.VMEM((512, 512), F32)],
        compiler_params=params(62),
        cost_estimate=lasts(11.5),
        name="feed_forward",
    )(*pieces, w_up, d_act)


def up_weight_kernel(left, right, out):
    value = dot_tn(left[...], right[...]).astype(BF)
    for z in range(4):
        out[z, 0] = value[z * 128 : (z + 1) * 128]


def up_weight_call(left, right):
    return pl.pallas_call(
        up_weight_kernel,
        grid=(4,),
        in_specs=[cols(512, 512), whole(512, 1024)],
        out_specs=pl.BlockSpec((4, 1, 128, 1024), lambda y: (0, y, 0, 0)),
        out_shape=like((4, 4, 128, 1024), BF),
        compiler_params=params(62),
        cost_estimate=lasts(1),
        name="up_weights",
    )(left, right)


def down_weight_kernel(info, left, right, o0, o1, o2, o3):
    value = dot_tn(left[...], right[...]).astype(BF)
    for s, out in enumerate((o0, o1, o2, o3)):

        @pl.when(pl.program_id(0) == s)
        def _():
            out[...] = value


def down_weight_call(info, left, right):
    return pl.pallas_call(
        down_weight_kernel,
        grid_spec=pltpu.PrefetchScalarGridSpec(
            num_scalar_prefetch=1,
            grid=(4,),
            in_specs=[
                pl.BlockSpec((512, 512), lambda s, info: (0, info[ORDER_Y + s])),
                pl.BlockSpec((512, 1024), lambda s, info: (0, 0)),
            ],
            out_specs=[pl.BlockSpec((512, 1024), lambda s, info: (0, 0))] * 4,
        ),
        out_shape=[like((512, 1024), BF)] * 4,
        compiler_params=params(62),
        cost_estimate=lasts(1),
        name="down_weights",
    )(info, left, right)


def sum_kernel(a, b, c, d, out):
    value = a[...].astype(F32) + b[...].astype(F32) + c[...].astype(F32) + d[...].astype(F32)
    out[...] = value.astype(BF)


def sum_call(parts, name):
    rows, n = parts[0].shape
    block = pl.BlockSpec((128, n), lambda i: (i, 0))
    return pl.pallas_call(
        sum_kernel,
        grid=(rows // 128,),
        in_specs=[block] * 4,
        out_specs=block,
        out_shape=like((rows, n), BF),
        compiler_params=params(62),
        cost_estimate=lasts(2),
        name=name,
    )(*parts)


def widen_kernel(got, query, key, value, gate):
    for i in range(4):
        part = got[2 * i].astype(F32) + got[2 * i + 1].astype(F32)
        gate[:, i * 256 : (i + 1) * 256] = part[:, :256]
        value[:, i * 256 : (i + 1) * 256] = part[:, 256:512]
        query[:, i * 128 : (i + 1) * 128] = part[:, 512:640]
        key[:, i * 128 : (i + 1) * 128] = part[:, 640:]


def widen_call(got):
    return pl.pallas_call(
        widen_kernel,
        out_shape=[like((64, 512), F32)] * 2 + [like((64, 1024), F32)] * 2,
        compiler_params=params(62),
        cost_estimate=lasts(400),
        name="projection_gradients",
    )(got)


def weight_kernel(info, *refs, order):
    lefts, rights, outs, total = refs[:8], refs[8:12], refs[12:-1], refs[-1]
    value = None
    for i in range(8):
        left, right = lefts[i], rights[i // 2]
        left = left[0] if len(left.shape) == 3 else left[...]
        rows = pl.ds((i % 2) * 256, 256)
        right = right[0, rows, :] if len(right.shape) == 3 else right[rows, :]
        part = dot(left, right)
        value = part if value is None else value + part
    if order is None:
        outs[0][...] = value.astype(BF).reshape(outs[0].shape)
        return
    total[...] = value.astype(BF)
    for s, out in enumerate(outs):
        out[...] = total[pl.ds(pl.multiple_of(info[order + s] * 128, 128), 128), :]


def weight_call(info, order, lefts, rights, name):
    def spec(value, rows, step):
        if not isinstance(value, tuple):
            n = value.shape[1]
            return pl.BlockSpec((rows, n), lambda i, info: (i * step, 0)), value
        value, place, known = value
        n = value.shape[2]
        if known:
            return pl.BlockSpec((1, rows, n), lambda i, info: (place, i * step, 0)), value
        return pl.BlockSpec((1, rows, n), lambda i, info: (info[place], i * step, 0)), value

    chosen = [spec(x, 512, 1) for x in lefts] + [spec(v, 512, 0) for v in rights]
    n, total_rows = chosen[-1][1].shape[-1], chosen[0][1].shape[-2]
    steps = total_rows // 512
    if order is None:
        out_specs = [pl.BlockSpec((4, 128, n), lambda i, info: (0, i, 0))]
        out_shape = [like((4, 128 * steps, n), BF)]
    else:
        out_specs = [pl.BlockSpec((128, n), lambda i, info: (i, 0))] * 4
        out_shape = [like((128 * steps, n), BF)] * 4
    return pl.pallas_call(
        functools.partial(weight_kernel, order=order),
        grid_spec=pltpu.PrefetchScalarGridSpec(
            num_scalar_prefetch=1,
            grid=(steps,),
            in_specs=[c[0] for c in chosen],
            out_specs=out_specs,
            scratch_shapes=[pltpu.VMEM((512, n), BF)],
        ),
        out_shape=out_shape,
        compiler_params=params(62),
        cost_estimate=lasts(8),
        name=name,
    )(info, *[c[1] for c in chosen])


def row_grad_kernel(dq, dk, dv, dg, wq, wk, wv, wg, p0, p1, p2, p3):
    total = dot_nt(dv[...], wv[...])
    total += dot_nt(dg[...], wg[...])
    total += dot_nt(dq[...], wq[...])
    total += dot_nt(dk[...], wk[...])
    for i, out in enumerate((p0, p1, p2, p3)):
        out[...] = total[i * 128 : (i + 1) * 128].astype(out.dtype)


def row_grad_call(grads, weights):
    return pl.pallas_call(
        row_grad_kernel,
        grid=(4,),
        in_specs=[whole(*g.shape) for g in grads]
        + [pl.BlockSpec((512, w.shape[1]), lambda i: (i, 0)) for w in weights],
        out_specs=[cols(128, 512)] * 4,
        out_shape=[like((128, 2048), BF)] * 4,
        compiler_params=params(62),
        cost_estimate=lasts(1),
        name="row_grad",
    )(*grads, *weights)


def shift_y(value, step):
    return lax.ppermute(
        value, "dp", [(i, ((i // 8 + step) % 4) * 8 + i % 8) for i in range(32)]
    )


def shift_z(value, step):
    return lax.ppermute(
        value,
        "dp",
        [(i, (i // 8) * 8 + ((i // 2 % 4 + step) % 4) * 2 + i % 2) for i in range(32)],
    )


def swap_xh(value):
    return lax.ppermute(value, "dp", [(i, i ^ 1) for i in range(32)])


def swap_xl(value):
    return lax.ppermute(value, "tensor", [(i, i ^ 2) for i in range(4)])


def swap_core(value):
    return lax.ppermute(value, "tensor", [(i, i ^ 1) for i in range(4)])


GROUPS_Y = [[y * 8 + r for y in range(4)] for r in range(8)]
GROUPS_Z = [[y * 8 + z * 2 + r for z in range(4)] for y in range(4) for r in range(2)]
GROUPS_YX = [[y * 8 + z * 2 + r for y in range(4) for r in range(2)] for z in range(4)]


def after(value, *others):
    return lax.optimization_barrier((value,) + others)[0]


def gather_row(own):
    across = swap_xl(own)
    return [own, across, swap_core(own), swap_core(across)]


def scatter_row(parts, hold=None):
    far = add_call(parts[1], swap_core(parts[3]))
    if hold is not None:
        far = after(far, hold)
    return (parts[0], swap_core(parts[2]), swap_xl(far)), far


def rows_of(value):
    return [value[i * 128 : (i + 1) * 128] for i in range(4)]


def piece(value, index, size, axis):
    return lax.dynamic_slice_in_dim(value, index * size, size, axis)


def send(values, shift):
    return [shift(v, step) for v, step in zip(values, SHIFTS)]


def exchange(values, groups):
    return lax.all_to_all(values, "dp", 0, 0, axis_index_groups=groups, tiled=True)


def reduce(part, groups):
    return lax.psum_scatter(part, "dp", scatter_dimension=0, axis_index_groups=groups, tiled=True)


def total(values):
    return sum(v.astype(F32) for v in values)


def local(
    tokens,
    segment_ids,
    norm1_gain,
    norm1_shift,
    w_query,
    w_key,
    w_value,
    w_gate,
    w_output,
    norm2_gain,
    norm2_shift,
    w_up,
    w_down,
    cotangent,
):
    tensor = lax.axis_index("tensor")
    dp = lax.axis_index("dp")
    zi, half_x = dp // 2 % 4, dp % 2
    info = device_info(dp // 8, zi, tensor)
    seg = segment_ids.reshape(4, 128)
    table = rotation_table()

    pieces = gather_row(after(tokens, info))
    hidden1, query, key, value, gate, group, factor, scores, gated = forward_call(
        info, pieces, norm1_gain, norm1_shift, w_query, w_key, w_value, w_gate, table, seg
    )
    cot = gather_row(after(cotangent, pieces[1]))

    part = dot(after(gated, cot[1]), w_output).astype(BF)
    row, sent = scatter_row(rows_of(part))
    hidden1_t = flip_call(after(hidden1[:128], sent), hidden1[128:256])
    hidden1_y = lax.all_gather(hidden1_t, "dp", axis_index_groups=GROUPS_Y)
    cot_all = after(jnp.concatenate(cot, axis=0), sent)
    mid_rows, hidden2_rows = middle_call(
        after(tokens, hidden1_t, cot_all), row, norm2_gain, norm2_shift
    )

    hidden2 = gather_row(hidden2_rows)
    d_act = dot_nt(after(cot_all, hidden2_rows), w_down)
    activated, d_up, hidden2_all, *parts = feed_forward_call(hidden2, w_up, d_act)
    row, sent = scatter_row(parts)
    begun = swap_core(sent[:16, :128])
    down_first = down_weight_call(info, after(cot_all, begun), after(activated, begun))
    down_y = [down_first[0]] + send(down_first[1:], shift_y)
    up_first = up_weight_call(after(hidden2_all, begun), d_up)
    up_part = reduce(up_first.reshape(2048, 1024), GROUPS_Z)
    d_mid, d_mid_low, sums2 = norm_back_call(
        row, after(mid_rows, down_first[0], up_first), norm2_gain, cotangent, "second_norm_back"
    )

    d_mid_pieces = gather_row(d_mid_low)
    hidden1_other = swap_core(after(hidden1_y, d_mid_low))
    back = backward_call(
        info, d_mid_pieces, after(w_output, up_first, hidden1_other), table, seg,
        (query, key, value, gate, group, factor, scores),
    )
    gv_y = [back[4]] + send(back[5:8], shift_y)
    qk_y = [back[8]] + send(back[9:12], shift_y)
    parts = list(row_grad_call(back[:4], (after(w_query, *down_y), w_key, w_value, w_gate)))
    d_mid_z = exchange(back[12], GROUPS_Z).reshape(4, 512, 256)
    parts[1] = after(parts[1], d_mid_z)
    row, sent = scatter_row(parts)
    gated_z = lax.all_gather(after(gated, sent), "dp", axis_index_groups=GROUPS_Z)

    lefts = [(x, SOURCE_Y + i, False) for i in range(4) for x in (hidden1_y, hidden1_other)]
    gv_y[0] = after(gv_y[0], sent)
    gv_parts = weight_call(info, ORDER_Z, lefts, gv_y, "gate_value_weights")
    gv_z = [gv_parts[0]] + send(gv_parts[1:], shift_z)
    tokens_grad, _, sums1 = norm_back_call(
        row, after(tokens, gv_parts[0]), norm1_gain, d_mid, "first_norm_back"
    )
    qk_y[0] = after(qk_y[0], gv_parts[0], tokens_grad)
    qk_parts = weight_call(info, ORDER_Z, lefts, qk_y, "query_key_weights")
    qk_z = [qk_parts[0]] + send(qk_parts[1:], shift_z)

    d_mid_z = after(d_mid_z, gv_parts[0])
    d_mid_other = swap_core(d_mid_z)
    down_half = sum_call([after(down_y[0], gv_parts[0])] + down_y[1:], "down_sum")
    down_part = total(exchange(down_half.reshape(4, 128, 1024), GROUPS_Z))
    lefts = [(x, i, True) for i in range(4) for x in (d_mid_z, d_mid_other)]
    rights = [(gated_z, i, True) for i in range(4)]
    output_parts = weight_call(info, ORDER_Y, lefts, rights, "output_weights")
    output_part = total([output_parts[0]] + send(output_parts[1:], shift_y))

    norm_parts = jnp.concatenate([sums1, sums2], axis=0).reshape(4, 128, 16)
    norm_parts = norm_parts.transpose(1, 0, 2).reshape(128, 64)
    norm_parts = lax.all_to_all(after(norm_parts, down_part), ("dp", "tensor"), 0, 0, tiled=True)
    norm_sums = jnp.sum(norm_parts, axis=0).reshape(4, 16)

    part = dot(after(activated, qk_parts[0]), w_down).astype(BF)
    row2, _ = scatter_row(rows_of(part), row[2])
    block_out = (mid_rows + total(row2)).astype(BF)

    ready = jnp.concatenate([sum_call(gv_z, "gate_value_sum"), sum_call(qk_z, "query_key_sum")], axis=1)
    got = exchange(after(ready.reshape(8, 64, 768), norm_sums), GROUPS_YX)
    def halves(part):
        mine = piece(part, half_x, 64, 0).astype(F32)
        return mine + swap_xh(piece(part, 1 - half_x, 64, 0).astype(BF)).astype(F32)

    up_sum = halves(reduce(after(up_part, gated_z), GROUPS_Y))
    output_sum, down_sum = halves(output_part).T, halves(down_part).T
    got = after(got, output_sum, down_sum, block_out)
    query_sum, key_sum, value_sum, gate_sum = widen_call(got)
    return (
        block_out,
        tokens_grad,
        norm_sums[0],
        norm_sums[1],
        query_sum,
        key_sum,
        value_sum,
        gate_sum,
        output_sum,
        norm_sums[2],
        norm_sums[3],
        up_sum,
        down_sum,
    )


def solution(mesh):
    in_specs = (
        P(("dp", "tensor"), None),
        P("dp"),
        P(),
        P(),
        P(None, "tensor"),
        P(None, "tensor"),
        P(None, "tensor"),
        P(None, "tensor"),
        P("tensor", None),
        P(),
        P(),
        P(None, "tensor"),
        P("tensor", None),
        P(("dp", "tensor"), None),
    )
    out_specs = (
        P(("dp", "tensor"), None),
        P(("dp", "tensor"), None),
        P(("dp", "tensor")),
        P(("dp", "tensor")),
        P("dp", "tensor"),
        P("dp", "tensor"),
        P("dp", "tensor"),
        P("dp", "tensor"),
        P("tensor", "dp"),
        P(("dp", "tensor")),
        P(("dp", "tensor")),
        P("dp", "tensor"),
        P("tensor", "dp"),
    )
    return jax.shard_map(local, mesh=mesh, in_specs=in_specs, out_specs=out_specs, check_vma=False)
```

```python
import functools

import jax
import jax.numpy as jnp
import numpy as np
from jax import lax
from jax.experimental import pallas as pl
from jax.experimental.pallas import tpu as pltpu
from jax.sharding import Mesh
from jax.sharding import PartitionSpec as P

DK = 256
DV = 512
F32 = jnp.float32
BF = jnp.bfloat16
SHIFTS = (1, -1, 2)


def dot(left, right):
    return jnp.dot(left, right, preferred_element_type=F32)


def dot_tn(left, right):
    return lax.dot_general(left, right, (((0,), (0,)), ((), ())), preferred_element_type=F32)


def dot_nt(left, right):
    return lax.dot_general(left, right, (((1,), (1,)), ((), ())), preferred_element_type=F32)


def norm_rows(value, epsilon):
    centred = value - jnp.mean(value, axis=-1, keepdims=True)
    factor = lax.rsqrt(jnp.mean(centred * centred, axis=-1, keepdims=True) + epsilon)
    return (centred * factor, factor)


def norm_back(grad, normed, factor):
    return factor * (
        grad
        - jnp.mean(grad, axis=-1, keepdims=True)
        - normed * jnp.mean(grad * normed, axis=-1, keepdims=True)
    )


def rotate(value, cosine, sine):
    half = DK // 2
    first = value[:, :half]
    second = value[:, half:]
    return jnp.concatenate(
        [first * cosine - second * sine, first * sine + second * cosine], axis=-1
    )


def rotation_table():
    half = DK // 2
    freqs = 10000.0 ** (-np.arange(half, dtype=np.float64) / half)
    angle = np.arange(512, dtype=np.float64)[:, None] * freqs[None, :]
    return np.concatenate([np.cos(angle), np.sin(angle)], axis=1).astype(np.float32)


def device_info(y, z, xl, c):
    tensor = xl * 2 + c
    k = np.zeros((5, 32), np.int32)
    k[0, PLACES : PLACES + 4], k[4, PLACES : PLACES + 4] = (0, 2, 1, 3), 1
    k[1, REL_Y : REL_Y + 4], k[3, REL_Y : REL_Y + 4], k[4, REL_Y : REL_Y + 4] = -1, range(4), 2
    for start, factor, steps in (
        (ORDER_Z, 2, (0, 1, 3, 2)), (SOURCE_Y, 1, (0, 3, 1, 2)),
    ):
        k[factor, start : start + 4], k[3, start : start + 4], k[4, start : start + 4] = 1, steps, 3
    added = (k[1] * y + k[2] * z + k[3]) & 3
    k[4, PARITY] = 4
    kinds = (tensor * 2, tensor ^ k[0], added ^ (added >> 1), added, z & 1)
    info = kinds[0]
    for i, value in enumerate(kinds[1:]):
        info = jnp.where(k[4] == i + 1, value, info)
    return info.astype(jnp.int32)


PLACES, REL_Y, ORDER_Z, SOURCE_Y, PARITY, HEAD = 0, 4, 8, 12, 16, 20
RATES = np.log1p(-(2.0 ** (-5.0 - np.arange(8)))).astype(np.float32)


PARAMS = pltpu.CompilerParams(vmem_limit_bytes=67_000_000)


def lasts(microseconds):
    return pl.CostEstimate(
        flops=int(microseconds * 0.3e9), bytes_accessed=100_000, transcendentals=0
    )


def whole(*shape):
    return pl.BlockSpec(shape, lambda i: (0,) * len(shape))


def cols(rows, n):
    return pl.BlockSpec((rows, n), lambda i: (0, i))


def scalars():
    return pl.BlockSpec(memory_space=pltpu.SMEM)


def like(shape, dtype):
    return jax.ShapeDtypeStruct(shape, dtype)


def decay_of(block, rate, info, seg_row, seg_t):
    rows = info[PLACES + block] * 128 + lax.broadcasted_iota(jnp.int32, (128, 512), 0)
    inner = lax.broadcasted_iota(jnp.int32, (1, 128), 1)
    columns = jnp.concatenate([info[PLACES + i] * 128 + inner for i in range(4)], axis=1)
    distance = rows - columns
    allowed = (seg_t[pl.ds(block * 128, 128), :1] == seg_row[...]) & (distance >= 0)
    steps_back = jnp.where(allowed, distance, 0).astype(F32)
    return jnp.where(allowed, jnp.exp(steps_back * rate), 0.0) * DK ** (-0.5)


def turn_of(block, info, table):
    rows = table[pl.ds(pl.multiple_of(info[PLACES + block] * 128, 128), 128), :]
    return rows[:, : DK // 2], rows[:, DK // 2 :]


def flip_row(info, seg, seg_row, seg_t):
    held = jnp.concatenate([seg[pl.ds(info[PLACES + i], 1), :] for i in range(4)], axis=1)
    held = held.astype(F32)
    seg_row[...] = held
    seg_t[...] = jnp.transpose(jnp.broadcast_to(held, (128, 512)))


def flip_into(out, first, column):
    for i in range(16):
        rows = pl.ds(i * 128, 128)
        out[rows, column : column + 128] = jnp.transpose(first[:, i * 128 : i * 128 + 128])


def start_copies(pairs, sems, first):
    copies = [
        pltpu.make_async_copy(source, place, sems.at[first + i])
        for i, (source, place) in enumerate(pairs)
    ]
    for copy in copies:
        copy.start()
    return copies


def forward_kernel(
    info, rates, gain, shift, table, seg, t0, t1, t2, t3, wq, wk, wv, wg, wo,
    h1_t, q, k, v, gate, group, factor, scores, gated, p0, p1, p2, p3,
    wq_, wk_, wv_, wg_, wo_, h1_t_, q_, k_, v_, gate_, group_, factor_, scores_, gated_,
    h1, seg_row, seg_t, pre, wide, pieces, sems,
):
    tokens = start_copies([(t, pieces.at[i]) for i, t in enumerate((t0, t1, t2, t3))], sems, 14)
    weights = start_copies(((wq, wq_), (wk, wk_), (wv, wv_), (wg, wg_), (wo, wo_)), sems, 0)
    flip_row(info, seg, seg_row, seg_t)
    for i, copy in enumerate(tokens):
        copy.wait()
        normed, _ = norm_rows(pieces[i].astype(F32), 1e-05)
        h1[pl.ds(i * 128, 128), :] = (normed * gain[...] + shift[...]).astype(BF)
    for copy, held, out in ((weights[0], wq_, q_), (weights[1], wk_, k_)):
        copy.wait()
        pre[...] = dot(h1[...], held[...])
        for i in range(4):
            rows = pl.ds(i * 128, 128)
            cosine, sine = turn_of(i, info, table)
            for h in range(2):
                heads = pl.ds(h * DK, DK)
                out[rows, heads] = rotate(pre[rows, heads], cosine, sine).astype(BF)
    weights[2].wait()
    v_[...] = dot(h1[...], wv_[...]).astype(BF)
    for i in range(2):
        flip_into(h1_t_, h1[pl.ds(i * 128, 128), :], i * 128)
    sent = start_copies(((h1_t_, h1_t), (q_, q), (k_, k), (v_, v)), sems, 5)
    weights[3].wait()
    for h in range(2):
        keys, vals = pl.ds(h * DK, DK), pl.ds(h * DV, DV)
        wide[...] = dot(h1[...], wg_[:, vals])
        gate_[:, vals] = wide[...].astype(BF)
        for i in range(4):
            rows = pl.ds(i * 128, 128)
            decay = decay_of(i, rates[info[HEAD] + h], info, seg_row, seg_t)
            score = (dot_nt(q_[rows, keys], k_[:, keys]) * decay).astype(BF)
            scores_[h, rows, :] = score
            normed, spread = norm_rows(dot(score, v_[:, vals]), 1.0)
            group_[rows, vals] = normed.astype(BF)
            factor_[rows, pl.ds(h * 128, 128)] = jnp.broadcast_to(spread, (128, 128))
            g = wide[rows, :]
            gated_[rows, vals] = (g * jax.nn.sigmoid(g) * normed).astype(BF)
    sent += start_copies(
        ((gate_, gate), (group_, group), (factor_, factor), (scores_, scores), (gated_, gated)), sems, 9
    )
    weights[4].wait()
    for i in range(4):
        columns = pl.ds(i * 512, 512)
        part = dot(gated_[...], wo_[:, columns]).astype(BF)
        for j, out in enumerate((p0, p1, p2, p3)):
            out[:, columns] = part[j * 128 : (j + 1) * 128]
    for copy in sent:
        copy.wait()


IN_PLACE = pl.BlockSpec(memory_space=pl.ANY)


def forward_call(info, pieces, gain, shift, wq, wk, wv, wg, wo, table, seg):
    kept = [
        ((2048, 256), BF), ((512, 512), BF), ((512, 512), BF), ((512, 1024), BF),
        ((512, 1024), BF), ((512, 1024), BF), ((512, 256), F32), ((2, 512, 512), BF),
        ((512, 1024), BF),
    ]
    weights = (wq, wk, wv, wg, wo)
    return pl.pallas_call(
        forward_kernel,
        in_specs=[scalars()] * 2
        + [pl.BlockSpec(memory_space=pltpu.VMEM)] * 4
        + [IN_PLACE] * 9,
        out_specs=[IN_PLACE] * 9 + [pl.BlockSpec(memory_space=pltpu.VMEM)] * 4,
        out_shape=[like(*s) for s in kept] + [like((128, 2048), BF)] * 4,
        scratch_shapes=[pltpu.VMEM(w.shape, BF) for w in weights]
        + [pltpu.VMEM(*s) for s in kept]
        + [
            pltpu.VMEM((512, 2048), BF), pltpu.VMEM((1, 512), F32), pltpu.VMEM((512, 128), F32),
            pltpu.VMEM((512, 512), F32), pltpu.VMEM((512, 512), F32), pltpu.VMEM((4, 128, 2048), BF),
            pltpu.SemaphoreType.DMA((18,)),
        ],
        compiler_params=PARAMS,
        cost_estimate=lasts(17),
        name="retention_forward",
    )(info, RATES, gain[None], shift[None], table, seg, *pieces, *weights)


def backward_kernel(
    info, rates, d0, d1, d2, d3, table, seg, wo, gate, group, factor, v, scores, k, q, wg, wv, wq, wk,
    y0, y1, y2, y3, p0, p1, p2, p3,
    wo_, gate_, group_, factor_, v_, scores_, k_, q_, weights, y_, full, grad, mixed, raw, pre, all_,
    seg_row, seg_t, sems,
):
    held = start_copies(
        (
            (wo, wo_), (group, group_), (gate, gate_), (factor, factor_), (v, v_), (k, k_),
            (scores, scores_), (q, q_),
        ),
        sems, 0,
    )
    late = start_copies(
        (
            (wg, weights.at[:, pl.ds(0, 1024)]), (wv, weights.at[:, pl.ds(1024, 1024)]),
            (wq, weights.at[:, pl.ds(2048, 512)]), (wk, weights.at[:, pl.ds(2560, 512)]),
        ),
        sems, 8,
    )
    flip_row(info, seg, seg_row, seg_t)
    for i, piece in enumerate((d0, d1, d2, d3)):
        full[pl.ds(i * 128, 128), :] = piece[...]
    sent = []
    for h in range(2):
        keys, vals = pl.ds(h * DK, DK), pl.ds(h * DV, DV)
        if h == 0:
            held[0].wait()
        grad[...] = dot_nt(full[...], wo_[vals, :])
        if h == 0:
            for copy in held[1:]:
                copy.wait()
        for i in range(4):
            rows = pl.ds(i * 128, 128)
            g, d = gate_[rows, vals].astype(F32), grad[rows, :]
            gn = group_[rows, vals].astype(F32)
            sig = jax.nn.sigmoid(g)
            silu = g * sig
            all_[rows, vals] = (d * gn * (sig + silu * (1.0 - sig))).astype(BF)
            spread = factor_[rows, pl.ds(h * 128, 128)][:, :1]
            dm = norm_back(d * silu, gn, spread).astype(BF)
            mixed[rows, :] = dm
            decay = decay_of(i, rates[info[HEAD] + h], info, seg_row, seg_t)
            dr = (dot_nt(dm, v_[:, vals]) * decay).astype(BF)
            raw[rows, :] = dr
            cosine, sine = turn_of(i, info, table)
            all_[rows, pl.ds(2048 + h * DK, DK)] = rotate(
                dot(dr, k_[:, keys]), cosine, -sine
            ).astype(BF)
        all_[:, pl.ds(1024 + h * DV, DV)] = dot_tn(scores_[h], mixed[...]).astype(BF)
        pre[...] = dot_tn(raw[...], q_[:, keys])
        for i in range(4):
            rows = pl.ds(i * 128, 128)
            cosine, sine = turn_of(i, info, table)
            all_[rows, pl.ds(2560 + h * DK, DK)] = rotate(pre[rows, :], cosine, -sine).astype(BF)
        for i in range(2):
            j = h * 2 + i
            for column, n, first in ((0, 256, 0), (256, 256, 1024), (512, 128, 2048), (640, 128, 2560)):
                y_[j, :, column : column + n] = all_[:, first + j * n : first + (j + 1) * n]
            for s, out in enumerate((y0, y1, y2, y3)):

                @pl.when(info[REL_Y + j] == s)
                def _():
                    pltpu.make_async_copy(y_.at[j], out, sems.at[12 + j]).start()

            sent.append(pltpu.make_async_copy(y_.at[j], y0, sems.at[12 + j]))
    for copy in late:
        copy.wait()
    for i in range(4):
        columns = pl.ds(i * 512, 512)
        part = dot_nt(all_[...], weights[columns, :]).astype(BF)
        for j, out in enumerate((p0, p1, p2, p3)):
            out[:, columns] = part[j * 128 : (j + 1) * 128]
    for copy in sent:
        copy.wait()


def backward_call(info, pieces, table, seg, wo, saved, wg, wv, wq, wk):
    q, k, v, gate, group, factor, scores = saved
    kept = (wo, gate, group, factor, v, scores, k, q)
    return pl.pallas_call(
        backward_kernel,
        in_specs=[scalars()] * 2
        + [pl.BlockSpec(memory_space=pltpu.VMEM)] * 6
        + [IN_PLACE] * 12,
        out_specs=[IN_PLACE] * 4 + [pl.BlockSpec(memory_space=pltpu.VMEM)] * 4,
        out_shape=[like((512, 768), BF)] * 4
        + [like((128, 2048), BF)] * 4,
        scratch_shapes=[pltpu.VMEM(x.shape, x.dtype) for x in kept]
        + [
            pltpu.VMEM((2048, 3072), BF), pltpu.VMEM((4, 512, 768), BF), pltpu.VMEM((512, 2048), BF),
            pltpu.VMEM((512, 512), F32), pltpu.VMEM((512, 512), BF), pltpu.VMEM((512, 512), BF),
            pltpu.VMEM((512, 256), F32), pltpu.VMEM((512, 3072), BF), pltpu.VMEM((1, 512), F32),
            pltpu.VMEM((512, 128), F32), pltpu.SemaphoreType.DMA((16,)),
        ],
        compiler_params=PARAMS,
        cost_estimate=lasts(100),
        name="retention_backward",
    )(info, RATES, *pieces, table, seg, *kept, wg, wv, wq, wk)


def middle_kernel(tokens, near, side, far, gain, shift, x2, h2):
    mid = tokens[...].astype(F32) + (near[...].astype(F32) + side[...].astype(F32))
    mid += far[...].astype(F32)
    x2[...] = mid
    normed, _ = norm_rows(mid, 1e-05)
    h2[...] = (normed * gain[...] + shift[...]).astype(BF)


def middle_call(tokens, row, gain, shift):
    return pl.pallas_call(
        middle_kernel,
        out_shape=[like((128, 2048), F32), like((128, 2048), BF)],
        compiler_params=PARAMS,
        cost_estimate=lasts(3),
        name="second_norm",
    )(tokens, *row, gain[None], shift[None])


def norm_back_kernel(near, side, far, rows, gain, outer, grad, sums, *low):
    d = near[...].astype(F32) + side[...].astype(F32) + far[...].astype(F32)
    normed, factor = norm_rows(rows[...].astype(F32), 1e-05)
    sums[0:1, :] = jnp.sum(d * normed, axis=0, keepdims=True)
    sums[1:2, :] = jnp.sum(d, axis=0, keepdims=True)
    total = outer[...].astype(F32) + norm_back(d * gain[...], normed, factor)
    grad[...] = total
    if low:
        low[0][...] = total.astype(BF)


def norm_back_call(row, rows, gain, outer, name, rounded=False):
    out_shape = [like((128, 2048), F32), like((2, 2048), F32)]
    if rounded:
        out_shape.append(like((128, 2048), BF))
    return pl.pallas_call(
        norm_back_kernel,
        out_shape=out_shape,
        compiler_params=PARAMS,
        cost_estimate=lasts(1),
        name=name,
    )(*row, rows, gain[None], outer)


def add_kernel(left, right, out, held, sems):
    copies = start_copies(((left, held.at[0]), (right, held.at[1])), sems, 0)
    for copy in copies:
        copy.wait()
    out[...] = (held[0].astype(F32) + held[1].astype(F32)).astype(BF)


def add_call(left, right):
    return pl.pallas_call(
        add_kernel,
        in_specs=[IN_PLACE] * 2,
        out_specs=pl.BlockSpec(memory_space=pltpu.VMEM),
        out_shape=like((128, 2048), BF),
        scratch_shapes=[pltpu.VMEM((2, 128, 2048), BF), pltpu.SemaphoreType.DMA((2,))],
        compiler_params=PARAMS,
        cost_estimate=lasts(2),
        name="chip_sum",
    )(left, right)


def cotangent_kernel(c0, c1, c2, c3, w_down, full, d_act):
    for i, piece in enumerate((c0, c1, c2, c3)):
        full[pl.ds(i * 128, 128), :] = piece[...]
    d_act[...] = dot_nt(full[...], w_down[...])


def cotangent_call(pieces, w_down):
    return pl.pallas_call(
        cotangent_kernel,
        grid=(2,),
        in_specs=[whole(128, 2048)] * 4 + [pl.BlockSpec((512, 2048), lambda f: (f, 0))],
        out_specs=[whole(512, 2048), cols(512, 512)],
        out_shape=[like((512, 2048), BF), like((512, 1024), F32)],
        compiler_params=PARAMS,
        cost_estimate=lasts(6),
        name="activation_grad",
    )(*pieces, w_down)


def down_kernel(act, w_down, p0, p1, p2, p3):
    part = dot(act[...], w_down[...]).astype(BF)
    for j, out in enumerate((p0, p1, p2, p3)):
        out[...] = part[j * 128 : (j + 1) * 128]


def down_call(act, w_down):
    return pl.pallas_call(
        down_kernel,
        grid=(2,),
        in_specs=[whole(512, 1024), cols(1024, 1024)],
        out_specs=[cols(128, 1024)] * 4,
        out_shape=[like((128, 2048), BF)] * 4,
        compiler_params=PARAMS,
        cost_estimate=lasts(1),
        name="down_projection",
    )(act, w_down)


def row_weight_kernel(left, right, out):
    value = dot_tn(left[...], right[...]).astype(BF)
    if len(out.shape) == 2:
        out[...] = value
    else:
        for z in range(4):
            out[z, 0] = value[z * 128 : (z + 1) * 128]


def row_weight_call(left, right, along, name):
    if along == "y":
        spec, shape = pl.BlockSpec((512, 1024), lambda y: (y, 0)), (2048, 1024)
    else:
        spec, shape = pl.BlockSpec((4, 1, 128, 1024), lambda y: (0, y, 0, 0)), (4, 4, 128, 1024)
    return pl.pallas_call(
        row_weight_kernel,
        grid=(4,),
        in_specs=[cols(512, 512), whole(512, 1024)],
        out_specs=spec,
        out_shape=like(shape, BF),
        compiler_params=PARAMS,
        cost_estimate=lasts(1),
        name=name,
    )(left, right).reshape(2048, 1024)


def feed_forward_kernel(
    h0, h1, h2, h3, w_up, d_act, act, d_up, full, p0, p1, p2, p3, total, pre,
):
    step = pl.program_id(0)

    @pl.when(step == 0)
    def _():
        for i, piece in enumerate((h0, h1, h2, h3)):
            full[pl.ds(i * 128, 128), :] = piece[...]

    pre[...] = dot(full[...], w_up[...])
    for i in range(4):
        rows = pl.ds(i * 128, 128)
        u = pre[rows, :]
        square = u * u
        t = jnp.tanh(0.7978845608 * (u + 0.044715 * u * square))
        act[rows, :] = (0.5 * u * (1.0 + t)).astype(BF)
        slope = 0.5 * (1.0 + t) + 0.5 * u * (1.0 - t * t) * 0.7978845608 * (
            1.0 + 3.0 * 0.044715 * square
        )
        d_up[rows, :] = (d_act[rows, :] * slope).astype(BF)

    outs = (p0, p1, p2, p3)

    @pl.when(step == 0)
    def _():
        total[...] = dot_nt(d_up[...], w_up[...])

    @pl.when(step == 1)
    def _():
        for i in range(4):
            columns = pl.ds(i * 512, 512)
            part = dot_nt(d_up[...], w_up[columns, :])
            for j in range(4):
                rows = pl.ds(j * 128, 128)
                value = part[j * 128 : (j + 1) * 128] + total[rows, columns]
                outs[j][:, columns] = value.astype(BF)


def feed_forward_call(pieces, w_up, d_act):
    return pl.pallas_call(
        feed_forward_kernel,
        grid=(2,),
        in_specs=[whole(128, 2048)] * 4 + [cols(2048, 512), cols(512, 512)],
        out_specs=[cols(512, 512)] * 2
        + [whole(512, 2048)]
        + [whole(128, 2048)] * 4,
        out_shape=[like((512, 1024), BF)] * 2
        + [like((512, 2048), BF)]
        + [like((128, 2048), BF)] * 4,
        scratch_shapes=[pltpu.VMEM((512, 2048), F32), pltpu.VMEM((512, 512), F32)],
        compiler_params=PARAMS,
        cost_estimate=lasts(1),
        name="feed_forward",
    )(*pieces, w_up, d_act)


def weight_kernel(info, *refs, sets, second, unread):
    count = sum(len(entries) + 4 for entries, _ in sets)
    outs, (held, right, total, sems) = refs[:-4], refs[-4:]
    at, first, copies, later, waits = 0, 0, [], [], []
    for j, (entries, width) in enumerate(sets):
        for s in range(4):
            place = right.at[pl.ds(s * 512, 512), pl.ds(first, width)]
            copies.append(pltpu.make_async_copy(refs[at], place, sems.at[at]))
            at += 1
        column = 0
        for entry in entries:
            source = refs[at].at[info[entry]]
            n = source.shape[1]
            for half, into in ((0, copies), (1, later)):
                rows = pl.ds(half * 1024, 1024)
                place = held.at[j, rows, pl.ds(column, n)]
                sem = sems.at[at + half * count]
                into.append(pltpu.make_async_copy(source.at[rows, :], place, sem))
            at, column = at + 1, column + n
        first += width
        waits.append((len(copies), len(later)))
    outs = outs[at + unread :]
    for copy in copies + later:
        copy.start()
    done, first = (0, 0), 0
    for j, (_, width) in enumerate(sets):
        for copy in copies[done[0] : waits[j][0]]:
            copy.wait()
        stop = first + width
        for b in range(4):
            if b == 2:
                for copy in later[done[1] : waits[j][1]]:
                    copy.wait()
            value = dot(held[j, pl.ds(b * 512, 512), :], right[:, first:stop]).astype(BF)
            if second == "z":
                total[:, first:stop] = value
                for s, out in enumerate(outs):
                    rows = pl.ds(pl.multiple_of(info[ORDER_Z + s] * 128, 128), 128)
                    out[pl.ds(b * 128, 128), first:stop] = total[rows, first:stop]
            else:
                for s, out in enumerate(outs):

                    @pl.when(info[REL_Y + b] == s)
                    def _():
                        out[:, first:stop] = value
        done, first = waits[j], stop


def weight_call(info, sets, second, name, others=()):
    operands, known = [], []
    for lefts, rights in sets:
        operands += [*rights, *(x for x, _ in lefts)]
        known.append(([entry for _, entry in lefts], rights[0].shape[1]))
    n = sum(width for _, width in known)
    out_shape = [like((512, n), BF)] * 4
    return pl.pallas_call(
        functools.partial(weight_kernel, sets=known, second=second, unread=len(others)),
        in_specs=[scalars()] + [IN_PLACE] * (len(operands) + len(others)),
        out_specs=[pl.BlockSpec(memory_space=pltpu.VMEM)] * len(out_shape),
        out_shape=out_shape,
        scratch_shapes=[
            pltpu.VMEM((len(sets), 2048, 2048), BF), pltpu.VMEM((2048, n), BF),
            pltpu.VMEM((512, n), BF), pltpu.SemaphoreType.DMA((2 * len(operands),)),
        ],
        compiler_params=PARAMS,
        cost_estimate=lasts(1),
        name=name,
    )(info, *operands, *others)


def output_weight_kernel(info, d0, d1, d2, d3, d4, d5, d6, d7, right, near, *refs):
    out, left = refs[-2:]

    @pl.when(pl.program_id(0) == 0)
    def _():
        for i, piece in enumerate((d0, d1, d2, d3, d4, d5, d6, d7)):
            for j in range(8):
                first = pl.multiple_of(j * 256 + info[PARITY] * 128, 128)
                left[pl.ds(i * 128, 128), pl.ds(j * 128, 128)] = piece[:, pl.ds(first, 128)]

    total = dot_tn(left[:512, :], right[...]) + dot_tn(left[512:, :], near[...])
    out[...] = total.astype(BF)


def output_weight_call(info, grads, rights, others=()):
    return pl.pallas_call(
        output_weight_kernel,
        grid=(2,),
        in_specs=[scalars()] + [whole(128, 2048)] * 8 + [cols(512, 512)] * 2 + [IN_PLACE] * len(others),
        out_specs=cols(1024, 512),
        out_shape=like((1024, 1024), BF),
        scratch_shapes=[pltpu.VMEM((1024, 1024), BF)],
        compiler_params=PARAMS,
        cost_estimate=lasts(1),
        name="output_weights",
    )(info, *grads, *rights, *others)


def sum_kernel(a, b, c, d, *refs):
    value = a[...].astype(F32) + b[...].astype(F32) + c[...].astype(F32) + d[...].astype(F32)
    refs[-1][...] = value.astype(BF)


def sum_call(parts, name, others=()):
    return pl.pallas_call(
        sum_kernel,
        in_specs=[pl.BlockSpec(memory_space=pltpu.VMEM)] * 4 + [IN_PLACE] * len(others),
        out_specs=pl.BlockSpec(memory_space=pltpu.VMEM),
        out_shape=like(parts[0].shape, BF),
        compiler_params=PARAMS,
        cost_estimate=lasts(2),
        name=name,
    )(*parts, *others)


def sum_joined_kernel(parts, out):
    value = parts[0].astype(F32) + parts[1].astype(F32)
    out[...] = value + parts[2].astype(F32) + parts[3].astype(F32)


def sum_joined_call(parts, name):
    return pl.pallas_call(
        sum_joined_kernel,
        out_shape=like(parts.shape[1:], F32),
        compiler_params=PARAMS,
        cost_estimate=lasts(1),
        name=name,
    )(parts)


def widen_kernel(got, query, key, value, gate):
    for i in range(4):
        part = got[2 * i].astype(F32) + got[2 * i + 1].astype(F32)
        wide, narrow = slice(i * 256, (i + 1) * 256), slice(i * 128, (i + 1) * 128)
        gate[:, wide], value[:, wide] = part[:, :256], part[:, 256:512]
        query[:, narrow], key[:, narrow] = part[:, 512:640], part[:, 640:]


def widen_call(got):
    return pl.pallas_call(
        widen_kernel,
        out_shape=[like((64, 512), F32)] * 2 + [like((64, 1024), F32)] * 2,
        compiler_params=PARAMS,
        cost_estimate=lasts(4),
        name="projection_gradients",
    )(got)


def arrived_kernel(*refs):
    refs[-1][...] = jnp.zeros(refs[-1].shape, F32)


def arrived_call(values, name, ahead):
    return pl.pallas_call(
        arrived_kernel,
        in_specs=[IN_PLACE] * len(values),
        out_specs=pl.BlockSpec(memory_space=pltpu.VMEM),
        out_shape=like((8, 128), F32),
        compiler_params=PARAMS,
        cost_estimate=lasts(ahead),
        name=name,
    )(*values)


DP, TENSOR = ("y", "z", "xh"), ("xl", "c")


def shift(value, axis, step):
    return lax.ppermute(value, axis, [(i, (i + step) % 4) for i in range(4)])


def swap(value, axis):
    return lax.ppermute(value, axis, [(0, 1), (1, 0)])


def pair(value, axis):
    return lax.ppermute(value, axis, [(i, i ^ 1) for i in range(4)])


def after(value, *others):
    return lax.optimization_barrier((value,) + others)[0]


def gather_row(own, *held):
    across = swap(own, "xl")
    return [own, across, swap(own, "c"), swap(after(across, *held), "c")]


def scatter_row(parts, hold=None):
    far = add_call(parts[1], swap(parts[3], "c"))
    if hold is not None:
        far = after(far, hold)
    return (parts[0], swap(after(parts[2], far), "c"), swap(far, "xl")), far


def send(values, axis):
    return [shift(v, axis, step) for v, step in zip(values, SHIFTS)]


def exchange(values, axes):
    return lax.all_to_all(values, axes, 0, 0, tiled=True)


def total(values):
    return sum(v.astype(F32) for v in values)


def local(
    tokens,
    segment_ids,
    norm1_gain,
    norm1_shift,
    w_query,
    w_key,
    w_value,
    w_gate,
    w_output,
    norm2_gain,
    norm2_shift,
    w_up,
    w_down,
    cotangent,
):
    info = device_info(
        lax.axis_index("y"), lax.axis_index("z"), lax.axis_index("xl"), lax.axis_index("c")
    )
    seg = segment_ids.reshape(4, 128)
    table = rotation_table()

    pieces = gather_row(after(tokens, info))
    hidden1_t, *saved, gated, p0, p1, p2, p3 = forward_call(
        info, pieces, norm1_gain, norm1_shift, w_query, w_key, w_value, w_gate, w_output, table, seg
    )
    cot = gather_row(after(cotangent, pieces[1]))
    row, sent = scatter_row((p0, p1, p2, after(p3, cot[1])))
    hidden1_y = lax.all_gather(after(hidden1_t, sent), "y")
    cot_all, d_act = cotangent_call((after(cot[0], sent), *cot[1:]), w_down)
    mid_rows, hidden2_rows = middle_call(after(tokens, d_act), row, norm2_gain, norm2_shift)

    gated_near = pair(after(gated, sent), "z")
    hidden2 = gather_row(hidden2_rows, gated_near)
    activated, d_up, hidden2_all, *parts = feed_forward_call(hidden2, w_up, d_act)
    row, sent = scatter_row(parts)
    up_first = row_weight_call(after(hidden2_all, row[1]), after(d_up, row[1]), "y", "up_weights")
    up_part = lax.psum_scatter(after(up_first, row[2]), "y", scatter_dimension=0, tiled=True)
    d_mid, sums2, d_mid_low = norm_back_call(
        row, after(mid_rows, up_first), norm2_gain, cotangent, "second_norm_back", True
    )

    begun = swap(d_mid_low[:16, :128], "c")
    down_first = row_weight_call(after(cot_all, begun), after(activated, begun), "z", "down_weights")
    hidden1_other = swap(after(hidden1_y, d_mid_low), "c")
    d_mid_pieces = gather_row(d_mid_low, down_first)
    near = [pair(d_mid_pieces[0], "z"), pair(d_mid_pieces[1], "z")]
    near += [swap(near[0], "c"), swap(near[1], "c")]
    back = backward_call(
        info, d_mid_pieces, table, seg, after(w_output, hidden1_other), saved,
        w_gate, w_value, w_query, w_key,
    )
    proj_y = [back[0]] + send(back[1:4], "y")
    row, sent = scatter_row((back[4], after(back[5], *near[:2]), *back[6:8]))
    down_part = lax.psum_scatter(after(down_first, sent, up_part), "z", scatter_dimension=0, tiled=True)

    half_x, z = lax.axis_index("xh"), lax.axis_index("z")

    def halves(part, index, move):
        size = part.shape[0] // 2
        mine = lax.dynamic_slice_in_dim(part, index * size, size, 0).astype(F32)
        other = lax.dynamic_slice_in_dim(part, (1 - index) * size, size, 0).astype(BF)
        return mine + move(other).astype(F32)

    def settle(part):
        return halves(part, half_x, lambda other: swap(other, "xh"))

    tokens_grad, sums1 = norm_back_call(row, tokens, norm1_gain, d_mid, "first_norm_back")
    out_parts = down_call(after(activated, sent), w_down)
    output_first = output_weight_call(info, (*d_mid_pieces, *near), (after(gated, tokens_grad), gated_near))
    output_part = exchange(output_first.reshape(4, 256, 1024), "y")
    output_part = sum_joined_call(output_part.reshape(4, 256, 1024), "output_sum")
    output_half = output_part

    norm_parts = jnp.concatenate([sums1, sums2], axis=0).reshape(4, 128, 16)
    norm_parts = norm_parts.transpose(1, 0, 2).reshape(128, 64)
    norm_got = exchange(norm_parts, DP + TENSOR)
    norm_sums = jnp.sum(norm_got, axis=0).reshape(4, 16)

    sides = [(x, SOURCE_Y + s) for s in range(4) for x in (hidden1_y, hidden1_other)]
    proj_y[0] = after(proj_y[0], tokens_grad)
    proj_parts = weight_call(
        info, [(sides, proj_y)], "z", "projection_weights", (out_parts[0], norm_got, arrived_call((*proj_y[1:], output_first), "rows_along_y", 12))
    )
    proj_z = [proj_parts[0]] + send(proj_parts[1:], "z")

    output_part = halves(after(output_part, proj_parts[0]), z // 2, lambda other: shift(other, "z", 2))
    down_part = lax.psum_scatter(down_part, "y", scatter_dimension=0, tiled=True)

    row, _ = scatter_row((out_parts[0], after(out_parts[1], proj_parts[0]), *out_parts[2:]))
    block_out = (mid_rows + total(row)).astype(BF)

    ready = sum_call(proj_z, "projection_sum", (output_half,))
    up_part = halves(after(up_part, ready), z // 2, lambda other: shift(other, "z", 2))
    up_part = halves(up_part, z % 2, lambda other: pair(other, "z"))
    got = exchange(ready.reshape(8, 64, 768), ("y", "xh"))
    query_sum, key_sum, value_sum, gate_sum = widen_call(got)
    return (
        block_out,
        tokens_grad,
        norm_sums[0],
        norm_sums[1],
        query_sum,
        key_sum,
        value_sum,
        gate_sum,
        settle(output_part).T,
        norm_sums[2],
        norm_sums[3],
        settle(up_part),
        settle(down_part).T,
    )


def solution(mesh):
    mesh = Mesh(mesh.devices.reshape(4, 4, 2, 2, 2), DP + TENSOR)
    in_specs = (
        P(DP + TENSOR, None),
        P(DP),
        P(),
        P(),
        P(None, TENSOR),
        P(None, TENSOR),
        P(None, TENSOR),
        P(None, TENSOR),
        P(TENSOR, None),
        P(),
        P(),
        P(None, TENSOR),
        P(TENSOR, None),
        P(DP + TENSOR, None),
    )
    out_specs = (
        P(DP + TENSOR, None),
        P(DP + TENSOR, None),
        P(DP + TENSOR),
        P(DP + TENSOR),
        P(DP, TENSOR),
        P(DP, TENSOR),
        P(DP, TENSOR),
        P(DP, TENSOR),
        P(TENSOR, DP),
        P(DP + TENSOR),
        P(DP + TENSOR),
        P(DP, TENSOR),
        P(TENSOR, DP),
    )
    return jax.shard_map(local, mesh=mesh, in_specs=in_specs, out_specs=out_specs, check_vma=False)
```

```python
import functools

import jax
import jax.numpy as jnp
import numpy as np
from jax import lax
from jax.experimental import pallas as pl
from jax.experimental.pallas import tpu as pltpu
from jax.sharding import Mesh
from jax.sharding import PartitionSpec as P

DK = 256
DV = 512
F32 = jnp.float32
BF = jnp.bfloat16
SHIFTS = (1, -1, 2)


def dot(left, right):
    return jnp.dot(left, right, preferred_element_type=F32)


def dot_tn(left, right):
    return lax.dot_general(left, right, (((0,), (0,)), ((), ())), preferred_element_type=F32)


def dot_nt(left, right):
    return lax.dot_general(left, right, (((1,), (1,)), ((), ())), preferred_element_type=F32)


def norm_rows(value, epsilon):
    centred = value - jnp.mean(value, axis=-1, keepdims=True)
    factor = lax.rsqrt(jnp.mean(centred * centred, axis=-1, keepdims=True) + epsilon)
    return (centred * factor, factor)


def norm_back(grad, normed, factor):
    return factor * (
        grad
        - jnp.mean(grad, axis=-1, keepdims=True)
        - normed * jnp.mean(grad * normed, axis=-1, keepdims=True)
    )


def rotate(value, cosine, sine):
    half = DK // 2
    first = value[:, :half]
    second = value[:, half:]
    return jnp.concatenate(
        [first * cosine - second * sine, first * sine + second * cosine], axis=-1
    )


def rotation_table():
    half = DK // 2
    freqs = 10000.0 ** (-np.arange(half, dtype=np.float64) / half)
    angle = np.arange(512, dtype=np.float64)[:, None] * freqs[None, :]
    return np.concatenate([np.cos(angle), np.sin(angle)], axis=1).astype(np.float32)


def device_info(y, z, xl, c):
    tensor = xl * 2 + c
    k = np.zeros((5, 32), np.int32)
    k[0, PLACES : PLACES + 4], k[4, PLACES : PLACES + 4] = (0, 2, 1, 3), 1
    k[1, REL_Y : REL_Y + 4], k[3, REL_Y : REL_Y + 4], k[4, REL_Y : REL_Y + 4] = -1, range(4), 2
    for start, factor, steps in (
        (ORDER_Z, 2, (0, 1, 3, 2)), (SOURCE_Y, 1, (0, 3, 1, 2)),
    ):
        k[factor, start : start + 4], k[3, start : start + 4], k[4, start : start + 4] = 1, steps, 3
    added = (k[1] * y + k[2] * z + k[3]) & 3
    k[4, PARITY] = 4
    kinds = (tensor * 2, tensor ^ k[0], added ^ (added >> 1), added, z & 1)
    info = kinds[0]
    for i, value in enumerate(kinds[1:]):
        info = jnp.where(k[4] == i + 1, value, info)
    return info.astype(jnp.int32)


PLACES, REL_Y, ORDER_Z, SOURCE_Y, PARITY, HEAD = 0, 4, 8, 12, 16, 20
RATES = np.log1p(-(2.0 ** (-5.0 - np.arange(8)))).astype(np.float32)


PARAMS = pltpu.CompilerParams(vmem_limit_bytes=67_000_000)


def lasts(microseconds):
    return pl.CostEstimate(
        flops=int(microseconds * 0.3e9), bytes_accessed=100_000, transcendentals=0
    )


def whole(*shape):
    return pl.BlockSpec(shape, lambda i: (0,) * len(shape))


def cols(rows, n):
    return pl.BlockSpec((rows, n), lambda i: (0, i))


def scalars():
    return pl.BlockSpec(memory_space=pltpu.SMEM)


def like(shape, dtype):
    return jax.ShapeDtypeStruct(shape, dtype)


def decay_of(block, rate, info, seg_row, seg_t):
    rows = info[PLACES + block] * 128 + lax.broadcasted_iota(jnp.int32, (128, 512), 0)
    inner = lax.broadcasted_iota(jnp.int32, (1, 128), 1)
    columns = jnp.concatenate([info[PLACES + i] * 128 + inner for i in range(4)], axis=1)
    distance = rows - columns
    allowed = (seg_t[pl.ds(block * 128, 128), :1] == seg_row[...]) & (distance >= 0)
    steps_back = jnp.where(allowed, distance, 0).astype(F32)
    return jnp.where(allowed, jnp.exp(steps_back * rate), 0.0) * DK ** (-0.5)


def turn_of(block, info, table):
    rows = table[pl.ds(pl.multiple_of(info[PLACES + block] * 128, 128), 128), :]
    return rows[:, : DK // 2], rows[:, DK // 2 :]


def flip_row(info, seg, seg_row, seg_t):
    held = jnp.concatenate([seg[pl.ds(info[PLACES + i], 1), :] for i in range(4)], axis=1)
    held = held.astype(F32)
    seg_row[...] = held
    seg_t[...] = jnp.transpose(jnp.broadcast_to(held, (128, 512)))


def flip_into(out, first, column):
    for i in range(16):
        rows = pl.ds(i * 128, 128)
        out[rows, column : column + 128] = jnp.transpose(first[:, i * 128 : i * 128 + 128])


def start_copies(pairs, sems, first):
    copies = [
        pltpu.make_async_copy(source, place, sems.at[first + i])
        for i, (source, place) in enumerate(pairs)
    ]
    for copy in copies:
        copy.start()
    return copies


def forward_kernel(
    info, rates, gain, shift, table, seg, t0, t1, t2, t3, wq, wk, wv, wg, wo,
    h1_t, q, k, v, gate, group, factor, scores, gated, p0, p1, p2, p3,
    wq_, wk_, wv_, wg_, wo_, h1_t_, q_, k_, v_, gate_, group_, factor_, scores_, gated_,
    h1, seg_row, seg_t, pre, wide, pieces, sems,
):
    tokens = start_copies([(t, pieces.at[i]) for i, t in enumerate((t0, t1, t2, t3))], sems, 14)
    weights = start_copies(((wq, wq_), (wk, wk_), (wv, wv_), (wg, wg_), (wo, wo_)), sems, 0)
    flip_row(info, seg, seg_row, seg_t)
    for i, copy in enumerate(tokens):
        copy.wait()
        normed, _ = norm_rows(pieces[i].astype(F32), 1e-05)
        h1[pl.ds(i * 128, 128), :] = (normed * gain[...] + shift[...]).astype(BF)
    for copy, held, out in ((weights[0], wq_, q_), (weights[1], wk_, k_)):
        copy.wait()
        pre[...] = dot(h1[...], held[...])
        for i in range(4):
            rows = pl.ds(i * 128, 128)
            cosine, sine = turn_of(i, info, table)
            for h in range(2):
                heads = pl.ds(h * DK, DK)
                out[rows, heads] = rotate(pre[rows, heads], cosine, sine).astype(BF)
    weights[2].wait()
    v_[...] = dot(h1[...], wv_[...]).astype(BF)
    for i in range(2):
        flip_into(h1_t_, h1[pl.ds(i * 128, 128), :], i * 128)
    sent = start_copies(((h1_t_, h1_t), (q_, q), (k_, k), (v_, v)), sems, 5)
    weights[3].wait()
    for h in range(2):
        keys, vals = pl.ds(h * DK, DK), pl.ds(h * DV, DV)
        wide[...] = dot(h1[...], wg_[:, vals])
        gate_[:, vals] = wide[...].astype(BF)
        for i in range(4):
            rows = pl.ds(i * 128, 128)
            decay = decay_of(i, rates[info[HEAD] + h], info, seg_row, seg_t)
            score = (dot_nt(q_[rows, keys], k_[:, keys]) * decay).astype(BF)
            scores_[h, rows, :] = score
            normed, spread = norm_rows(dot(score, v_[:, vals]), 1.0)
            group_[rows, vals] = normed.astype(BF)
            factor_[rows, pl.ds(h * 128, 128)] = jnp.broadcast_to(spread, (128, 128))
            g = wide[rows, :]
            gated_[rows, vals] = (g * jax.nn.sigmoid(g) * normed).astype(BF)
    sent += start_copies(
        ((gate_, gate), (group_, group), (factor_, factor), (scores_, scores), (gated_, gated)), sems, 9
    )
    weights[4].wait()
    for i in range(4):
        columns = pl.ds(i * 512, 512)
        part = dot(gated_[...], wo_[:, columns]).astype(BF)
        for j, out in enumerate((p0, p1, p2, p3)):
            out[:, columns] = part[j * 128 : (j + 1) * 128]
    for copy in sent:
        copy.wait()


IN_PLACE = pl.BlockSpec(memory_space=pl.ANY)


def forward_call(info, pieces, gain, shift, wq, wk, wv, wg, wo, table, seg):
    kept = [
        ((2048, 256), BF), ((512, 512), BF), ((512, 512), BF), ((512, 1024), BF),
        ((512, 1024), BF), ((512, 1024), BF), ((512, 256), F32), ((2, 512, 512), BF),
        ((512, 1024), BF),
    ]
    weights = (wq, wk, wv, wg, wo)
    return pl.pallas_call(
        forward_kernel,
        in_specs=[scalars()] * 2
        + [pl.BlockSpec(memory_space=pltpu.VMEM)] * 4
        + [IN_PLACE] * 9,
        out_specs=[IN_PLACE] * 9 + [pl.BlockSpec(memory_space=pltpu.VMEM)] * 4,
        out_shape=[like(*s) for s in kept] + [like((128, 2048), BF)] * 4,
        scratch_shapes=[pltpu.VMEM(w.shape, BF) for w in weights]
        + [pltpu.VMEM(*s) for s in kept]
        + [
            pltpu.VMEM((512, 2048), BF), pltpu.VMEM((1, 512), F32), pltpu.VMEM((512, 128), F32),
            pltpu.VMEM((512, 512), F32), pltpu.VMEM((512, 512), F32), pltpu.VMEM((4, 128, 2048), BF),
            pltpu.SemaphoreType.DMA((18,)),
        ],
        compiler_params=PARAMS,
        cost_estimate=lasts(17),
        name="retention_forward",
    )(info, RATES, gain[None], shift[None], table, seg, *pieces, *weights)


def backward_kernel(
    info, rates, d0, d1, d2, d3, table, seg, wo, gate, group, factor, v, scores, k, q, wg, wv, wq, wk,
    y0, y1, y2, y3, p0, p1, p2, p3,
    wo_, gate_, group_, factor_, v_, scores_, k_, q_, weights, y_, full, grad, mixed, raw, pre, all_,
    seg_row, seg_t, sems,
):
    held = start_copies(
        (
            (wo, wo_), (group, group_), (gate, gate_), (factor, factor_), (v, v_), (k, k_),
            (scores, scores_), (q, q_),
        ),
        sems, 0,
    )
    late = start_copies(
        (
            (wg, weights.at[:, pl.ds(0, 1024)]), (wv, weights.at[:, pl.ds(1024, 1024)]),
            (wq, weights.at[:, pl.ds(2048, 512)]), (wk, weights.at[:, pl.ds(2560, 512)]),
        ),
        sems, 8,
    )
    flip_row(info, seg, seg_row, seg_t)
    for i, piece in enumerate((d0, d1, d2, d3)):
        full[pl.ds(i * 128, 128), :] = piece[...]
    sent = []
    for h in range(2):
        keys, vals = pl.ds(h * DK, DK), pl.ds(h * DV, DV)
        if h == 0:
            held[0].wait()
        grad[...] = dot_nt(full[...], wo_[vals, :])
        if h == 0:
            for copy in held[1:]:
                copy.wait()
        for i in range(4):
            rows = pl.ds(i * 128, 128)
            g, d = gate_[rows, vals].astype(F32), grad[rows, :]
            gn = group_[rows, vals].astype(F32)
            sig = jax.nn.sigmoid(g)
            silu = g * sig
            all_[rows, vals] = (d * gn * (sig + silu * (1.0 - sig))).astype(BF)
            spread = factor_[rows, pl.ds(h * 128, 128)][:, :1]
            dm = norm_back(d * silu, gn, spread).astype(BF)
            mixed[rows, :] = dm
            decay = decay_of(i, rates[info[HEAD] + h], info, seg_row, seg_t)
            dr = (dot_nt(dm, v_[:, vals]) * decay).astype(BF)
            raw[rows, :] = dr
            cosine, sine = turn_of(i, info, table)
            all_[rows, pl.ds(2048 + h * DK, DK)] = rotate(
                dot(dr, k_[:, keys]), cosine, -sine
            ).astype(BF)
        all_[:, pl.ds(1024 + h * DV, DV)] = dot_tn(scores_[h], mixed[...]).astype(BF)
        pre[...] = dot_tn(raw[...], q_[:, keys])
        for i in range(4):
            rows = pl.ds(i * 128, 128)
            cosine, sine = turn_of(i, info, table)
            all_[rows, pl.ds(2560 + h * DK, DK)] = rotate(pre[rows, :], cosine, -sine).astype(BF)
        for i in range(2):
            j = h * 2 + i
            for column, n, first in ((0, 256, 0), (256, 256, 1024), (512, 128, 2048), (640, 128, 2560)):
                y_[j, :, column : column + n] = all_[:, first + j * n : first + (j + 1) * n]
            for s, out in enumerate((y0, y1, y2, y3)):

                @pl.when(info[REL_Y + j] == s)
                def _():
                    pltpu.make_async_copy(y_.at[j], out, sems.at[12 + j]).start()

            sent.append(pltpu.make_async_copy(y_.at[j], y0, sems.at[12 + j]))
    for copy in late:
        copy.wait()
    for i in range(4):
        columns = pl.ds(i * 512, 512)
        part = dot_nt(all_[...], weights[columns, :]).astype(BF)
        for j, out in enumerate((p0, p1, p2, p3)):
            out[:, columns] = part[j * 128 : (j + 1) * 128]
    for copy in sent:
        copy.wait()


def backward_call(info, pieces, table, seg, wo, saved, wg, wv, wq, wk):
    q, k, v, gate, group, factor, scores = saved
    kept = (wo, gate, group, factor, v, scores, k, q)
    return pl.pallas_call(
        backward_kernel,
        in_specs=[scalars()] * 2
        + [pl.BlockSpec(memory_space=pltpu.VMEM)] * 6
        + [IN_PLACE] * 12,
        out_specs=[IN_PLACE] * 4 + [pl.BlockSpec(memory_space=pltpu.VMEM)] * 4,
        out_shape=[like((512, 768), BF)] * 4
        + [like((128, 2048), BF)] * 4,
        scratch_shapes=[pltpu.VMEM(x.shape, x.dtype) for x in kept]
        + [
            pltpu.VMEM((2048, 3072), BF), pltpu.VMEM((4, 512, 768), BF), pltpu.VMEM((512, 2048), BF),
            pltpu.VMEM((512, 512), F32), pltpu.VMEM((512, 512), BF), pltpu.VMEM((512, 512), BF),
            pltpu.VMEM((512, 256), F32), pltpu.VMEM((512, 3072), BF), pltpu.VMEM((1, 512), F32),
            pltpu.VMEM((512, 128), F32), pltpu.SemaphoreType.DMA((16,)),
        ],
        compiler_params=PARAMS,
        cost_estimate=lasts(100),
        name="retention_backward",
    )(info, RATES, *pieces, table, seg, *kept, wg, wv, wq, wk)


def middle_kernel(tokens, near, side, far, gain, shift, x2, h2):
    mid = tokens[...].astype(F32) + (near[...].astype(F32) + side[...].astype(F32))
    mid += far[...].astype(F32)
    x2[...] = mid
    normed, _ = norm_rows(mid, 1e-05)
    h2[...] = (normed * gain[...] + shift[...]).astype(BF)


def middle_call(tokens, row, gain, shift):
    return pl.pallas_call(
        middle_kernel,
        out_shape=[like((128, 2048), F32), like((128, 2048), BF)],
        compiler_params=PARAMS,
        cost_estimate=lasts(3),
        name="second_norm",
    )(tokens, *row, gain[None], shift[None])


def norm_back_kernel(near, side, far, rows, gain, outer, grad, sums, *low):
    d = near[...].astype(F32) + side[...].astype(F32) + far[...].astype(F32)
    normed, factor = norm_rows(rows[...].astype(F32), 1e-05)
    sums[0:1, :] = jnp.sum(d * normed, axis=0, keepdims=True)
    sums[1:2, :] = jnp.sum(d, axis=0, keepdims=True)
    total = outer[...].astype(F32) + norm_back(d * gain[...], normed, factor)
    grad[...] = total
    if low:
        low[0][...] = total.astype(BF)


def norm_back_call(row, rows, gain, outer, name, rounded=False):
    out_shape = [like((128, 2048), F32), like((2, 2048), F32)]
    if rounded:
        out_shape.append(like((128, 2048), BF))
    return pl.pallas_call(
        norm_back_kernel,
        out_shape=out_shape,
        compiler_params=PARAMS,
        cost_estimate=lasts(1),
        name=name,
    )(*row, rows, gain[None], outer)


def add_kernel(left, right, out, held, sems):
    copies = start_copies(((left, held.at[0]), (right, held.at[1])), sems, 0)
    for copy in copies:
        copy.wait()
    out[...] = (held[0].astype(F32) + held[1].astype(F32)).astype(BF)


def add_call(left, right):
    return pl.pallas_call(
        add_kernel,
        in_specs=[IN_PLACE] * 2,
        out_specs=pl.BlockSpec(memory_space=pltpu.VMEM),
        out_shape=like((128, 2048), BF),
        scratch_shapes=[pltpu.VMEM((2, 128, 2048), BF), pltpu.SemaphoreType.DMA((2,))],
        compiler_params=PARAMS,
        cost_estimate=lasts(2),
        name="chip_sum",
    )(left, right)


def cotangent_kernel(c0, c1, c2, c3, w_down, full, d_act):
    for i, piece in enumerate((c0, c1, c2, c3)):
        full[pl.ds(i * 128, 128), :] = piece[...]
    d_act[...] = dot_nt(full[...], w_down[...])


def cotangent_call(pieces, w_down):
    return pl.pallas_call(
        cotangent_kernel,
        grid=(2,),
        in_specs=[whole(128, 2048)] * 4 + [pl.BlockSpec((512, 2048), lambda f: (f, 0))],
        out_specs=[whole(512, 2048), cols(512, 512)],
        out_shape=[like((512, 2048), BF), like((512, 1024), F32)],
        compiler_params=PARAMS,
        cost_estimate=lasts(6),
        name="activation_grad",
    )(*pieces, w_down)


def down_kernel(act, w_down, p0, p1, p2, p3):
    part = dot(act[...], w_down[...]).astype(BF)
    for j, out in enumerate((p0, p1, p2, p3)):
        out[...] = part[j * 128 : (j + 1) * 128]


def down_call(act, w_down):
    return pl.pallas_call(
        down_kernel,
        grid=(2,),
        in_specs=[whole(512, 1024), cols(1024, 1024)],
        out_specs=[cols(128, 1024)] * 4,
        out_shape=[like((128, 2048), BF)] * 4,
        compiler_params=PARAMS,
        cost_estimate=lasts(1),
        name="down_projection",
    )(act, w_down)


def row_weight_kernel(left, right, out):
    value = dot_tn(left[...], right[...]).astype(BF)
    if len(out.shape) == 2:
        out[...] = value
    else:
        for z in range(4):
            out[z, 0] = value[z * 128 : (z + 1) * 128]


def row_weight_call(left, right, along, name):
    if along == "y":
        spec, shape = pl.BlockSpec((512, 1024), lambda y: (y, 0)), (2048, 1024)
    else:
        spec, shape = pl.BlockSpec((4, 1, 128, 1024), lambda y: (0, y, 0, 0)), (4, 4, 128, 1024)
    return pl.pallas_call(
        row_weight_kernel,
        grid=(4,),
        in_specs=[cols(512, 512), whole(512, 1024)],
        out_specs=spec,
        out_shape=like(shape, BF),
        compiler_params=PARAMS,
        cost_estimate=lasts(1),
        name=name,
    )(left, right).reshape(2048, 1024)


def feed_forward_kernel(
    h0, h1, h2, h3, w_up, d_act, act, d_up, full, p0, p1, p2, p3, total, pre,
):
    step = pl.program_id(0)

    @pl.when(step == 0)
    def _():
        for i, piece in enumerate((h0, h1, h2, h3)):
            full[pl.ds(i * 128, 128), :] = piece[...]

    pre[...] = dot(full[...], w_up[...])
    for i in range(4):
        rows = pl.ds(i * 128, 128)
        u = pre[rows, :]
        square = u * u
        t = jnp.tanh(0.7978845608 * (u + 0.044715 * u * square))
        act[rows, :] = (0.5 * u * (1.0 + t)).astype(BF)
        slope = 0.5 * (1.0 + t) + 0.5 * u * (1.0 - t * t) * 0.7978845608 * (
            1.0 + 3.0 * 0.044715 * square
        )
        d_up[rows, :] = (d_act[rows, :] * slope).astype(BF)

    outs = (p0, p1, p2, p3)

    @pl.when(step == 0)
    def _():
        total[...] = dot_nt(d_up[...], w_up[...])

    @pl.when(step == 1)
    def _():
        for i in range(4):
            columns = pl.ds(i * 512, 512)
            part = dot_nt(d_up[...], w_up[columns, :])
            for j in range(4):
                rows = pl.ds(j * 128, 128)
                value = part[j * 128 : (j + 1) * 128] + total[rows, columns]
                outs[j][:, columns] = value.astype(BF)


def feed_forward_call(pieces, w_up, d_act):
    return pl.pallas_call(
        feed_forward_kernel,
        grid=(2,),
        in_specs=[whole(128, 2048)] * 4 + [cols(2048, 512), cols(512, 512)],
        out_specs=[cols(512, 512)] * 2
        + [whole(512, 2048)]
        + [whole(128, 2048)] * 4,
        out_shape=[like((512, 1024), BF)] * 2
        + [like((512, 2048), BF)]
        + [like((128, 2048), BF)] * 4,
        scratch_shapes=[pltpu.VMEM((512, 2048), F32), pltpu.VMEM((512, 512), F32)],
        compiler_params=PARAMS,
        cost_estimate=lasts(1),
        name="feed_forward",
    )(*pieces, w_up, d_act)


def weight_kernel(info, *refs, sets, second, unread):
    count = sum(len(entries) + 4 for entries, _ in sets)
    outs, (held, right, total, sems) = refs[:-4], refs[-4:]
    at, first, copies, later, waits = 0, 0, [], [], []
    for j, (entries, width) in enumerate(sets):
        for s in range(4):
            place = right.at[pl.ds(s * 512, 512), pl.ds(first, width)]
            copies.append(pltpu.make_async_copy(refs[at], place, sems.at[at]))
            at += 1
        column = 0
        for entry in entries:
            source = refs[at].at[info[entry]]
            n = source.shape[1]
            for half, into in ((0, copies), (1, later)):
                rows = pl.ds(half * 1024, 1024)
                place = held.at[j, rows, pl.ds(column, n)]
                sem = sems.at[at + half * count]
                into.append(pltpu.make_async_copy(source.at[rows, :], place, sem))
            at, column = at + 1, column + n
        first += width
        waits.append((len(copies), len(later)))
    outs = outs[at + unread :]
    for copy in copies + later:
        copy.start()
    done, first = (0, 0), 0
    for j, (_, width) in enumerate(sets):
        for copy in copies[done[0] : waits[j][0]]:
            copy.wait()
        stop = first + width
        for b in range(4):
            if b == 2:
                for copy in later[done[1] : waits[j][1]]:
                    copy.wait()
            value = dot(held[j, pl.ds(b * 512, 512), :], right[:, first:stop]).astype(BF)
            if second == "z":
                total[:, first:stop] = value
                for s, out in enumerate(outs):
                    rows = pl.ds(pl.multiple_of(info[ORDER_Z + s] * 128, 128), 128)
                    out[pl.ds(b * 128, 128), first:stop] = total[rows, first:stop]
            else:
                for s, out in enumerate(outs):

                    @pl.when(info[REL_Y + b] == s)
                    def _():
                        out[:, first:stop] = value
        done, first = waits[j], stop


def weight_call(info, sets, second, name, others=()):
    operands, known = [], []
    for lefts, rights in sets:
        operands += [*rights, *(x for x, _ in lefts)]
        known.append(([entry for _, entry in lefts], rights[0].shape[1]))
    n = sum(width for _, width in known)
    out_shape = [like((512, n), BF)] * 4
    return pl.pallas_call(
        functools.partial(weight_kernel, sets=known, second=second, unread=len(others)),
        in_specs=[scalars()] + [IN_PLACE] * (len(operands) + len(others)),
        out_specs=[pl.BlockSpec(memory_space=pltpu.VMEM)] * len(out_shape),
        out_shape=out_shape,
        scratch_shapes=[
            pltpu.VMEM((len(sets), 2048, 2048), BF), pltpu.VMEM((2048, n), BF),
            pltpu.VMEM((512, n), BF), pltpu.SemaphoreType.DMA((2 * len(operands),)),
        ],
        compiler_params=PARAMS,
        cost_estimate=lasts(1),
        name=name,
    )(info, *operands, *others)


def output_weight_kernel(info, d0, d1, d2, d3, d4, d5, d6, d7, right, near, *refs):
    out, left = refs[-2:]

    @pl.when(pl.program_id(0) == 0)
    def _():
        for i, piece in enumerate((d0, d1, d2, d3, d4, d5, d6, d7)):
            for j in range(8):
                first = pl.multiple_of(j * 256 + info[PARITY] * 128, 128)
                left[pl.ds(i * 128, 128), pl.ds(j * 128, 128)] = piece[:, pl.ds(first, 128)]

    total = dot_tn(left[:512, :], right[...]) + dot_tn(left[512:, :], near[...])
    out[...] = total.astype(BF)


def output_weight_call(info, grads, rights, others=()):
    return pl.pallas_call(
        output_weight_kernel,
        grid=(2,),
        in_specs=[scalars()] + [whole(128, 2048)] * 8 + [cols(512, 512)] * 2 + [IN_PLACE] * len(others),
        out_specs=cols(1024, 512),
        out_shape=like((1024, 1024), BF),
        scratch_shapes=[pltpu.VMEM((1024, 1024), BF)],
        compiler_params=PARAMS,
        cost_estimate=lasts(1),
        name="output_weights",
    )(info, *grads, *rights, *others)


def sum_kernel(a, b, c, d, *refs):
    value = a[...].astype(F32) + b[...].astype(F32) + c[...].astype(F32) + d[...].astype(F32)
    refs[-1][...] = value.astype(BF)


def sum_call(parts, name, others=()):
    return pl.pallas_call(
        sum_kernel,
        in_specs=[pl.BlockSpec(memory_space=pltpu.VMEM)] * 4 + [IN_PLACE] * len(others),
        out_specs=pl.BlockSpec(memory_space=pltpu.VMEM),
        out_shape=like(parts[0].shape, BF),
        compiler_params=PARAMS,
        cost_estimate=lasts(2),
        name=name,
    )(*parts, *others)


def sum_joined_kernel(parts, out):
    value = parts[0].astype(F32) + parts[1].astype(F32)
    out[...] = value + parts[2].astype(F32) + parts[3].astype(F32)


def sum_joined_call(parts, name):
    return pl.pallas_call(
        sum_joined_kernel,
        out_shape=like(parts.shape[1:], F32),
        compiler_params=PARAMS,
        cost_estimate=lasts(1),
        name=name,
    )(parts)


def widen_kernel(got, query, key, value, gate):
    for i in range(4):
        part = got[2 * i].astype(F32) + got[2 * i + 1].astype(F32)
        wide, narrow = slice(i * 256, (i + 1) * 256), slice(i * 128, (i + 1) * 128)
        gate[:, wide], value[:, wide] = part[:, :256], part[:, 256:512]
        query[:, narrow], key[:, narrow] = part[:, 512:640], part[:, 640:]


def widen_call(got):
    return pl.pallas_call(
        widen_kernel,
        out_shape=[like((64, 512), F32)] * 2 + [like((64, 1024), F32)] * 2,
        compiler_params=PARAMS,
        cost_estimate=lasts(4),
        name="projection_gradients",
    )(got)


def arrived_kernel(*refs):
    refs[-1][...] = jnp.zeros(refs[-1].shape, F32)


def arrived_call(values, name, ahead):
    return pl.pallas_call(
        arrived_kernel,
        in_specs=[IN_PLACE] * len(values),
        out_specs=pl.BlockSpec(memory_space=pltpu.VMEM),
        out_shape=like((8, 128), F32),
        compiler_params=PARAMS,
        cost_estimate=lasts(ahead),
        name=name,
    )(*values)


DP, TENSOR = ("y", "z", "xh"), ("xl", "c")


def shift(value, axis, step):
    return lax.ppermute(value, axis, [(i, (i + step) % 4) for i in range(4)])


def swap(value, axis):
    return lax.ppermute(value, axis, [(0, 1), (1, 0)])


def pair(value, axis):
    return lax.ppermute(value, axis, [(i, i ^ 1) for i in range(4)])


def after(value, *others):
    return lax.optimization_barrier((value,) + others)[0]


def gather_row(own, *held):
    across = swap(own, "xl")
    return [own, across, swap(own, "c"), swap(after(across, *held), "c")]


def scatter_row(parts, hold=None):
    far = add_call(parts[1], swap(parts[3], "c"))
    if hold is not None:
        far = after(far, hold)
    return (parts[0], swap(after(parts[2], far), "c"), swap(far, "xl")), far


def send(values, axis):
    return [shift(v, axis, step) for v, step in zip(values, SHIFTS)]


def exchange(values, axes):
    return lax.all_to_all(values, axes, 0, 0, tiled=True)


def total(values):
    return sum(v.astype(F32) for v in values)


def local(
    tokens,
    segment_ids,
    norm1_gain,
    norm1_shift,
    w_query,
    w_key,
    w_value,
    w_gate,
    w_output,
    norm2_gain,
    norm2_shift,
    w_up,
    w_down,
    cotangent,
):
    info = device_info(
        lax.axis_index("y"), lax.axis_index("z"), lax.axis_index("xl"), lax.axis_index("c")
    )
    seg = segment_ids.reshape(4, 128)
    table = rotation_table()

    pieces = gather_row(after(tokens, info))
    hidden1_t, *saved, gated, p0, p1, p2, p3 = forward_call(
        info, pieces, norm1_gain, norm1_shift, w_query, w_key, w_value, w_gate, w_output, table, seg
    )
    cot = gather_row(after(cotangent, pieces[1]))
    row, sent = scatter_row((p0, p1, p2, after(p3, cot[1])))
    hidden1_y = lax.all_gather(after(hidden1_t, sent), "y")
    cot_all, d_act = cotangent_call((after(cot[0], sent), *cot[1:]), w_down)
    mid_rows, hidden2_rows = middle_call(after(tokens, d_act), row, norm2_gain, norm2_shift)

    gated_near = pair(after(gated, sent), "z")
    hidden2 = gather_row(hidden2_rows, gated_near)
    activated, d_up, hidden2_all, *parts = feed_forward_call(hidden2, w_up, d_act)
    row, sent = scatter_row(parts)
    up_first = row_weight_call(after(hidden2_all, row[1]), after(d_up, row[1]), "y", "up_weights")
    up_part = lax.psum_scatter(after(up_first, row[2]), "y", scatter_dimension=0, tiled=True)
    d_mid, sums2, d_mid_low = norm_back_call(
        row, after(mid_rows, up_first), norm2_gain, cotangent, "second_norm_back", True
    )

    begun = swap(d_mid_low[:16, :128], "c")
    down_first = row_weight_call(after(cot_all, begun), after(activated, begun), "z", "down_weights")
    hidden1_other = swap(after(hidden1_y, d_mid_low), "c")
    d_mid_pieces = gather_row(d_mid_low, down_first)
    near = [pair(d_mid_pieces[0], "z"), pair(d_mid_pieces[1], "z")]
    near += [swap(near[0], "c"), swap(near[1], "c")]
    back = backward_call(
        info, d_mid_pieces, table, seg, after(w_output, hidden1_other), saved,
        w_gate, w_value, w_query, w_key,
    )
    proj_y = [back[0]] + send(back[1:4], "y")
    row, sent = scatter_row((back[4], after(back[5], *near[:2]), *back[6:8]))
    down_part = lax.psum_scatter(after(down_first, sent, up_part), "z", scatter_dimension=0, tiled=True)

    half_x, z = lax.axis_index("xh"), lax.axis_index("z")

    def halves(part, index, move):
        size = part.shape[0] // 2
        mine = lax.dynamic_slice_in_dim(part, index * size, size, 0).astype(F32)
        other = lax.dynamic_slice_in_dim(part, (1 - index) * size, size, 0).astype(BF)
        return mine + move(other).astype(F32)

    def settle(part):
        return halves(part, half_x, lambda other: swap(other, "xh"))

    tokens_grad, sums1 = norm_back_call(row, tokens, norm1_gain, d_mid, "first_norm_back")
    output_first = output_weight_call(info, (*d_mid_pieces, *near), (after(gated, tokens_grad), gated_near))
    output_part = exchange(output_first.reshape(4, 256, 1024), "y")
    output_part = sum_joined_call(output_part.reshape(4, 256, 1024), "output_sum")
    output_half = output_part

    norm_parts = jnp.concatenate([sums1, sums2], axis=0).reshape(4, 128, 16)
    norm_parts = norm_parts.transpose(1, 0, 2).reshape(128, 64)
    norm_got = exchange(norm_parts, DP + TENSOR)
    norm_sums = jnp.sum(norm_got, axis=0).reshape(4, 16)

    sides = [(x, SOURCE_Y + s) for s in range(4) for x in (hidden1_y, hidden1_other)]
    proj_y[0] = after(proj_y[0], tokens_grad)
    proj_parts = weight_call(
        info, [(sides, proj_y)], "z", "projection_weights", (norm_got, arrived_call((*proj_y[1:], output_first), "rows_along_y", 12))
    )
    proj_z = [proj_parts[0]] + send(proj_parts[1:], "z")

    output_part = halves(after(output_part, proj_parts[0]), z // 2, lambda other: shift(other, "z", 2))
    down_part = lax.psum_scatter(down_part, "y", scatter_dimension=0, tiled=True)

    out_parts = down_call(after(activated, proj_parts[0]), w_down)
    row, _ = scatter_row((out_parts[0], after(out_parts[1], proj_parts[0]), *out_parts[2:]))
    block_out = (mid_rows + total(row)).astype(BF)

    ready = sum_call(proj_z, "projection_sum", (output_half,))
    up_part = halves(after(up_part, ready), z // 2, lambda other: shift(other, "z", 2))
    up_part = halves(up_part, z % 2, lambda other: pair(other, "z"))
    got = exchange(ready.reshape(8, 64, 768), ("y", "xh"))
    query_sum, key_sum, value_sum, gate_sum = widen_call(got)
    return (
        block_out,
        tokens_grad,
        norm_sums[0],
        norm_sums[1],
        query_sum,
        key_sum,
        value_sum,
        gate_sum,
        settle(output_part).T,
        norm_sums[2],
        norm_sums[3],
        settle(up_part),
        settle(down_part).T,
    )


def solution(mesh):
    mesh = Mesh(mesh.devices.reshape(4, 4, 2, 2, 2), DP + TENSOR)
    in_specs = (
        P(DP + TENSOR, None),
        P(DP),
        P(),
        P(),
        P(None, TENSOR),
        P(None, TENSOR),
        P(None, TENSOR),
        P(None, TENSOR),
        P(TENSOR, None),
        P(),
        P(),
        P(None, TENSOR),
        P(TENSOR, None),
        P(DP + TENSOR, None),
    )
    out_specs = (
        P(DP + TENSOR, None),
        P(DP + TENSOR, None),
        P(DP + TENSOR),
        P(DP + TENSOR),
        P(DP, TENSOR),
        P(DP, TENSOR),
        P(DP, TENSOR),
        P(DP, TENSOR),
        P(TENSOR, DP),
        P(DP + TENSOR),
        P(DP + TENSOR),
        P(DP, TENSOR),
        P(TENSOR, DP),
    )
    return jax.shard_map(local, mesh=mesh, in_specs=in_specs, out_specs=out_specs, check_vma=False)
```

```python
import functools

import jax
import jax.numpy as jnp
import numpy as np
from jax import lax
from jax.experimental import pallas as pl
from jax.experimental.pallas import tpu as pltpu
from jax.sharding import Mesh
from jax.sharding import PartitionSpec as P

DK = 256
DV = 512
F32 = jnp.float32
BF = jnp.bfloat16
SHIFTS = (1, -1, 2)


def dot(left, right):
    return jnp.dot(left, right, preferred_element_type=F32)


def dot_tn(left, right):
    return lax.dot_general(left, right, (((0,), (0,)), ((), ())), preferred_element_type=F32)


def dot_nt(left, right):
    return lax.dot_general(left, right, (((1,), (1,)), ((), ())), preferred_element_type=F32)


def norm_rows(value, epsilon):
    centred = value - jnp.mean(value, axis=-1, keepdims=True)
    factor = lax.rsqrt(jnp.mean(centred * centred, axis=-1, keepdims=True) + epsilon)
    return (centred * factor, factor)


def norm_back(grad, normed, factor):
    return factor * (
        grad
        - jnp.mean(grad, axis=-1, keepdims=True)
        - normed * jnp.mean(grad * normed, axis=-1, keepdims=True)
    )


def rotate(value, cosine, sine):
    half = DK // 2
    first = value[:, :half]
    second = value[:, half:]
    return jnp.concatenate(
        [first * cosine - second * sine, first * sine + second * cosine], axis=-1
    )


def rotation_table():
    half = DK // 2
    freqs = 10000.0 ** (-np.arange(half, dtype=np.float64) / half)
    angle = np.arange(512, dtype=np.float64)[:, None] * freqs[None, :]
    return np.concatenate([np.cos(angle), np.sin(angle)], axis=1).astype(np.float32)


def device_info(y, z, xl, c):
    tensor = xl * 2 + c
    k = np.zeros((5, 32), np.int32)
    k[0, PLACES : PLACES + 4], k[4, PLACES : PLACES + 4] = (0, 2, 1, 3), 1
    k[1, REL_Y : REL_Y + 4], k[3, REL_Y : REL_Y + 4], k[4, REL_Y : REL_Y + 4] = -1, range(4), 2
    for start, factor, steps in (
        (ORDER_Z, 2, (0, 1, 3, 2)), (SOURCE_Y, 1, (0, 3, 1, 2)),
    ):
        k[factor, start : start + 4], k[3, start : start + 4], k[4, start : start + 4] = 1, steps, 3
    added = (k[1] * y + k[2] * z + k[3]) & 3
    k[4, PARITY] = 4
    kinds = (tensor * 2, tensor ^ k[0], added ^ (added >> 1), added, z & 1)
    info = kinds[0]
    for i, value in enumerate(kinds[1:]):
        info = jnp.where(k[4] == i + 1, value, info)
    return info.astype(jnp.int32)


PLACES, REL_Y, ORDER_Z, SOURCE_Y, PARITY, HEAD = 0, 4, 8, 12, 16, 20
RATES = np.log1p(-(2.0 ** (-5.0 - np.arange(8)))).astype(np.float32)


PARAMS = pltpu.CompilerParams(vmem_limit_bytes=67_000_000)


def lasts(microseconds):
    return pl.CostEstimate(
        flops=int(microseconds * 0.3e9), bytes_accessed=100_000, transcendentals=0
    )


def whole(*shape):
    return pl.BlockSpec(shape, lambda i: (0,) * len(shape))


def cols(rows, n):
    return pl.BlockSpec((rows, n), lambda i: (0, i))


def scalars():
    return pl.BlockSpec(memory_space=pltpu.SMEM)


def like(shape, dtype):
    return jax.ShapeDtypeStruct(shape, dtype)


def decay_of(block, rate, info, seg_row, seg_t):
    rows = info[PLACES + block] * 128 + lax.broadcasted_iota(jnp.int32, (128, 512), 0)
    inner = lax.broadcasted_iota(jnp.int32, (1, 128), 1)
    columns = jnp.concatenate([info[PLACES + i] * 128 + inner for i in range(4)], axis=1)
    distance = rows - columns
    allowed = (seg_t[pl.ds(block * 128, 128), :1] == seg_row[...]) & (distance >= 0)
    steps_back = jnp.where(allowed, distance, 0).astype(F32)
    return jnp.where(allowed, jnp.exp(steps_back * rate), 0.0) * DK ** (-0.5)


def turn_of(block, info, table):
    rows = table[pl.ds(pl.multiple_of(info[PLACES + block] * 128, 128), 128), :]
    return rows[:, : DK // 2], rows[:, DK // 2 :]


def flip_row(info, seg, seg_row, seg_t):
    held = jnp.concatenate([seg[pl.ds(info[PLACES + i], 1), :] for i in range(4)], axis=1)
    held = held.astype(F32)
    seg_row[...] = held
    seg_t[...] = jnp.transpose(jnp.broadcast_to(held, (128, 512)))


def flip_into(out, first, column):
    for i in range(16):
        rows = pl.ds(i * 128, 128)
        out[rows, column : column + 128] = jnp.transpose(first[:, i * 128 : i * 128 + 128])


def start_copies(pairs, sems, first):
    copies = [
        pltpu.make_async_copy(source, place, sems.at[first + i])
        for i, (source, place) in enumerate(pairs)
    ]
    for copy in copies:
        copy.start()
    return copies


def forward_kernel(
    info, rates, gain, shift, table, seg, t0, t1, t2, t3, wq, wk, wv, wg, wo,
    h1_t, q, k, v, gate, group, factor, scores, gated, p0, p1, p2, p3,
    wq_, wk_, wv_, wg_, wo_, h1_t_, q_, k_, v_, gate_, group_, factor_, scores_, gated_,
    h1, seg_row, seg_t, pre, wide, pieces, sems,
):
    tokens = start_copies([(t, pieces.at[i]) for i, t in enumerate((t0, t1, t2, t3))], sems, 14)
    weights = start_copies(((wq, wq_), (wk, wk_), (wv, wv_), (wg, wg_), (wo, wo_)), sems, 0)
    flip_row(info, seg, seg_row, seg_t)
    for i, copy in enumerate(tokens):
        copy.wait()
        normed, _ = norm_rows(pieces[i].astype(F32), 1e-05)
        h1[pl.ds(i * 128, 128), :] = (normed * gain[...] + shift[...]).astype(BF)
    for copy, held, out in ((weights[0], wq_, q_), (weights[1], wk_, k_)):
        copy.wait()
        pre[...] = dot(h1[...], held[...])
        for i in range(4):
            rows = pl.ds(i * 128, 128)
            cosine, sine = turn_of(i, info, table)
            for h in range(2):
                heads = pl.ds(h * DK, DK)
                out[rows, heads] = rotate(pre[rows, heads], cosine, sine).astype(BF)
    weights[2].wait()
    v_[...] = dot(h1[...], wv_[...]).astype(BF)
    for i in range(2):
        flip_into(h1_t_, h1[pl.ds(i * 128, 128), :], i * 128)
    sent = start_copies(((h1_t_, h1_t), (q_, q), (k_, k), (v_, v)), sems, 5)
    weights[3].wait()
    for h in range(2):
        keys, vals = pl.ds(h * DK, DK), pl.ds(h * DV, DV)
        wide[...] = dot(h1[...], wg_[:, vals])
        gate_[:, vals] = wide[...].astype(BF)
        for i in range(4):
            rows = pl.ds(i * 128, 128)
            decay = decay_of(i, rates[info[HEAD] + h], info, seg_row, seg_t)
            score = (dot_nt(q_[rows, keys], k_[:, keys]) * decay).astype(BF)
            scores_[h, rows, :] = score
            normed, spread = norm_rows(dot(score, v_[:, vals]), 1.0)
            group_[rows, vals] = normed.astype(BF)
            factor_[rows, pl.ds(h * 128, 128)] = jnp.broadcast_to(spread, (128, 128))
            g = wide[rows, :]
            gated_[rows, vals] = (g * jax.nn.sigmoid(g) * normed).astype(BF)
    sent += start_copies(
        ((gate_, gate), (group_, group), (factor_, factor), (scores_, scores), (gated_, gated)), sems, 9
    )
    weights[4].wait()
    for i in range(4):
        columns = pl.ds(i * 512, 512)
        part = dot(gated_[...], wo_[:, columns]).astype(BF)
        for j, out in enumerate((p0, p1, p2, p3)):
            out[:, columns] = part[j * 128 : (j + 1) * 128]
    for copy in sent:
        copy.wait()


IN_PLACE = pl.BlockSpec(memory_space=pl.ANY)


def forward_call(info, pieces, gain, shift, wq, wk, wv, wg, wo, table, seg):
    kept = [
        ((2048, 256), BF), ((512, 512), BF), ((512, 512), BF), ((512, 1024), BF),
        ((512, 1024), BF), ((512, 1024), BF), ((512, 256), F32), ((2, 512, 512), BF),
        ((512, 1024), BF),
    ]
    weights = (wq, wk, wv, wg, wo)
    return pl.pallas_call(
        forward_kernel,
        in_specs=[scalars()] * 2
        + [pl.BlockSpec(memory_space=pltpu.VMEM)] * 4
        + [IN_PLACE] * 9,
        out_specs=[IN_PLACE] * 9 + [pl.BlockSpec(memory_space=pltpu.VMEM)] * 4,
        out_shape=[like(*s) for s in kept] + [like((128, 2048), BF)] * 4,
        scratch_shapes=[pltpu.VMEM(w.shape, BF) for w in weights]
        + [pltpu.VMEM(*s) for s in kept]
        + [
            pltpu.VMEM((512, 2048), BF), pltpu.VMEM((1, 512), F32), pltpu.VMEM((512, 128), F32),
            pltpu.VMEM((512, 512), F32), pltpu.VMEM((512, 512), F32), pltpu.VMEM((4, 128, 2048), BF),
            pltpu.SemaphoreType.DMA((18,)),
        ],
        compiler_params=PARAMS,
        cost_estimate=lasts(17),
        name="retention_forward",
    )(info, RATES, gain[None], shift[None], table, seg, *pieces, *weights)


def backward_kernel(
    info, rates, d0, d1, d2, d3, table, seg, wo, gate, group, factor, v, scores, k, q, wg, wv, wq, wk,
    y0, y1, y2, y3, p0, p1, p2, p3,
    wo_, gate_, group_, factor_, v_, scores_, k_, q_, weights, y_, full, grad, mixed, raw, pre, all_,
    seg_row, seg_t, sems,
):
    held = start_copies(
        (
            (wo, wo_), (group, group_), (gate, gate_), (factor, factor_), (v, v_), (k, k_),
            (scores, scores_), (q, q_),
        ),
        sems, 0,
    )
    late = start_copies(
        (
            (wg, weights.at[:, pl.ds(0, 1024)]), (wv, weights.at[:, pl.ds(1024, 1024)]),
            (wq, weights.at[:, pl.ds(2048, 512)]), (wk, weights.at[:, pl.ds(2560, 512)]),
        ),
        sems, 8,
    )
    flip_row(info, seg, seg_row, seg_t)
    for i, piece in enumerate((d0, d1, d2, d3)):
        full[pl.ds(i * 128, 128), :] = piece[...]
    sent = []
    for h in range(2):
        keys, vals = pl.ds(h * DK, DK), pl.ds(h * DV, DV)
        if h == 0:
            held[0].wait()
        grad[...] = dot_nt(full[...], wo_[vals, :])
        if h == 0:
            for copy in held[1:]:
                copy.wait()
        for i in range(4):
            rows = pl.ds(i * 128, 128)
            g, d = gate_[rows, vals].astype(F32), grad[rows, :]
            gn = group_[rows, vals].astype(F32)
            sig = jax.nn.sigmoid(g)
            silu = g * sig
            all_[rows, vals] = (d * gn * (sig + silu * (1.0 - sig))).astype(BF)
            spread = factor_[rows, pl.ds(h * 128, 128)][:, :1]
            dm = norm_back(d * silu, gn, spread).astype(BF)
            mixed[rows, :] = dm
            decay = decay_of(i, rates[info[HEAD] + h], info, seg_row, seg_t)
            dr = (dot_nt(dm, v_[:, vals]) * decay).astype(BF)
            raw[rows, :] = dr
            cosine, sine = turn_of(i, info, table)
            all_[rows, pl.ds(2048 + h * DK, DK)] = rotate(
                dot(dr, k_[:, keys]), cosine, -sine
            ).astype(BF)
        all_[:, pl.ds(1024 + h * DV, DV)] = dot_tn(scores_[h], mixed[...]).astype(BF)
        pre[...] = dot_tn(raw[...], q_[:, keys])
        for i in range(4):
            rows = pl.ds(i * 128, 128)
            cosine, sine = turn_of(i, info, table)
            all_[rows, pl.ds(2560 + h * DK, DK)] = rotate(pre[rows, :], cosine, -sine).astype(BF)
        for i in range(2):
            j = h * 2 + i
            for column, n, first in ((0, 256, 0), (256, 256, 1024), (512, 128, 2048), (640, 128, 2560)):
                y_[j, :, column : column + n] = all_[:, first + j * n : first + (j + 1) * n]
            for s, out in enumerate((y0, y1, y2, y3)):

                @pl.when(info[REL_Y + j] == s)
                def _():
                    pltpu.make_async_copy(y_.at[j], out, sems.at[12 + j]).start()

            sent.append(pltpu.make_async_copy(y_.at[j], y0, sems.at[12 + j]))
    for copy in late:
        copy.wait()
    for i in range(4):
        columns = pl.ds(i * 512, 512)
        part = dot_nt(all_[...], weights[columns, :]).astype(BF)
        for j, out in enumerate((p0, p1, p2, p3)):
            out[:, columns] = part[j * 128 : (j + 1) * 128]
    for copy in sent:
        copy.wait()


def backward_call(info, pieces, table, seg, wo, saved, wg, wv, wq, wk):
    q, k, v, gate, group, factor, scores = saved
    kept = (wo, gate, group, factor, v, scores, k, q)
    return pl.pallas_call(
        backward_kernel,
        in_specs=[scalars()] * 2
        + [pl.BlockSpec(memory_space=pltpu.VMEM)] * 6
        + [IN_PLACE] * 12,
        out_specs=[IN_PLACE] * 4 + [pl.BlockSpec(memory_space=pltpu.VMEM)] * 4,
        out_shape=[like((512, 768), BF)] * 4
        + [like((128, 2048), BF)] * 4,
        scratch_shapes=[pltpu.VMEM(x.shape, x.dtype) for x in kept]
        + [
            pltpu.VMEM((2048, 3072), BF), pltpu.VMEM((4, 512, 768), BF), pltpu.VMEM((512, 2048), BF),
            pltpu.VMEM((512, 512), F32), pltpu.VMEM((512, 512), BF), pltpu.VMEM((512, 512), BF),
            pltpu.VMEM((512, 256), F32), pltpu.VMEM((512, 3072), BF), pltpu.VMEM((1, 512), F32),
            pltpu.VMEM((512, 128), F32), pltpu.SemaphoreType.DMA((16,)),
        ],
        compiler_params=PARAMS,
        cost_estimate=lasts(100),
        name="retention_backward",
    )(info, RATES, *pieces, table, seg, *kept, wg, wv, wq, wk)


def middle_kernel(tokens, near, side, far, gain, shift, x2, h2):
    mid = tokens[...].astype(F32) + (near[...].astype(F32) + side[...].astype(F32))
    mid += far[...].astype(F32)
    x2[...] = mid
    normed, _ = norm_rows(mid, 1e-05)
    h2[...] = (normed * gain[...] + shift[...]).astype(BF)


def middle_call(tokens, row, gain, shift):
    return pl.pallas_call(
        middle_kernel,
        out_shape=[like((128, 2048), F32), like((128, 2048), BF)],
        compiler_params=PARAMS,
        cost_estimate=lasts(3),
        name="second_norm",
    )(tokens, *row, gain[None], shift[None])


def norm_back_kernel(near, side, far, rows, gain, outer, grad, sums, *low):
    d = near[...].astype(F32) + side[...].astype(F32) + far[...].astype(F32)
    normed, factor = norm_rows(rows[...].astype(F32), 1e-05)
    sums[0:1, :] = jnp.sum(d * normed, axis=0, keepdims=True)
    sums[1:2, :] = jnp.sum(d, axis=0, keepdims=True)
    total = outer[...].astype(F32) + norm_back(d * gain[...], normed, factor)
    grad[...] = total
    if low:
        low[0][...] = total.astype(BF)


def norm_back_call(row, rows, gain, outer, name, rounded=False):
    out_shape = [like((128, 2048), F32), like((2, 2048), F32)]
    if rounded:
        out_shape.append(like((128, 2048), BF))
    return pl.pallas_call(
        norm_back_kernel,
        out_shape=out_shape,
        compiler_params=PARAMS,
        cost_estimate=lasts(1),
        name=name,
    )(*row, rows, gain[None], outer)


def add_kernel(left, right, out, held, sems):
    copies = start_copies(((left, held.at[0]), (right, held.at[1])), sems, 0)
    for copy in copies:
        copy.wait()
    out[...] = (held[0].astype(F32) + held[1].astype(F32)).astype(BF)


def add_call(left, right):
    return pl.pallas_call(
        add_kernel,
        in_specs=[IN_PLACE] * 2,
        out_specs=pl.BlockSpec(memory_space=pltpu.VMEM),
        out_shape=like((128, 2048), BF),
        scratch_shapes=[pltpu.VMEM((2, 128, 2048), BF), pltpu.SemaphoreType.DMA((2,))],
        compiler_params=PARAMS,
        cost_estimate=lasts(2),
        name="chip_sum",
    )(left, right)


def cotangent_kernel(c0, c1, c2, c3, w_down, full, d_act):
    for i, piece in enumerate((c0, c1, c2, c3)):
        full[pl.ds(i * 128, 128), :] = piece[...]
    d_act[...] = dot_nt(full[...], w_down[...])


def cotangent_call(pieces, w_down):
    return pl.pallas_call(
        cotangent_kernel,
        grid=(2,),
        in_specs=[whole(128, 2048)] * 4 + [pl.BlockSpec((512, 2048), lambda f: (f, 0))],
        out_specs=[whole(512, 2048), cols(512, 512)],
        out_shape=[like((512, 2048), BF), like((512, 1024), F32)],
        compiler_params=PARAMS,
        cost_estimate=lasts(6),
        name="activation_grad",
    )(*pieces, w_down)


def down_kernel(act, w_down, p0, p1, p2, p3):
    part = dot(act[...], w_down[...]).astype(BF)
    for j, out in enumerate((p0, p1, p2, p3)):
        out[...] = part[j * 128 : (j + 1) * 128]


def down_call(act, w_down):
    return pl.pallas_call(
        down_kernel,
        grid=(2,),
        in_specs=[whole(512, 1024), cols(1024, 1024)],
        out_specs=[cols(128, 1024)] * 4,
        out_shape=[like((128, 2048), BF)] * 4,
        compiler_params=PARAMS,
        cost_estimate=lasts(1),
        name="down_projection",
    )(act, w_down)


def row_weight_kernel(left, right, out):
    value = dot_tn(left[...], right[...]).astype(BF)
    if len(out.shape) == 2:
        out[...] = value
    else:
        for z in range(4):
            out[z, 0] = value[z * 128 : (z + 1) * 128]


def row_weight_call(left, right, along, name):
    if along == "y":
        spec, shape = pl.BlockSpec((512, 1024), lambda y: (y, 0)), (2048, 1024)
    else:
        spec, shape = pl.BlockSpec((4, 1, 128, 1024), lambda y: (0, y, 0, 0)), (4, 4, 128, 1024)
    return pl.pallas_call(
        row_weight_kernel,
        grid=(4,),
        in_specs=[cols(512, 512), whole(512, 1024)],
        out_specs=spec,
        out_shape=like(shape, BF),
        compiler_params=PARAMS,
        cost_estimate=lasts(1),
        name=name,
    )(left, right).reshape(2048, 1024)


def feed_forward_kernel(
    h0, h1, h2, h3, w_up, d_act, act, d_up, full, p0, p1, p2, p3, total, pre,
):
    step = pl.program_id(0)

    @pl.when(step == 0)
    def _():
        for i, piece in enumerate((h0, h1, h2, h3)):
            full[pl.ds(i * 128, 128), :] = piece[...]

    pre[...] = dot(full[...], w_up[...])
    for i in range(4):
        rows = pl.ds(i * 128, 128)
        u = pre[rows, :]
        square = u * u
        t = jnp.tanh(0.7978845608 * (u + 0.044715 * u * square))
        act[rows, :] = (0.5 * u * (1.0 + t)).astype(BF)
        slope = 0.5 * (1.0 + t) + 0.5 * u * (1.0 - t * t) * 0.7978845608 * (
            1.0 + 3.0 * 0.044715 * square
        )
        d_up[rows, :] = (d_act[rows, :] * slope).astype(BF)

    outs = (p0, p1, p2, p3)

    @pl.when(step == 0)
    def _():
        total[...] = dot_nt(d_up[...], w_up[...])

    @pl.when(step == 1)
    def _():
        for i in range(4):
            columns = pl.ds(i * 512, 512)
            part = dot_nt(d_up[...], w_up[columns, :])
            for j in range(4):
                rows = pl.ds(j * 128, 128)
                value = part[j * 128 : (j + 1) * 128] + total[rows, columns]
                outs[j][:, columns] = value.astype(BF)


def feed_forward_call(pieces, w_up, d_act):
    return pl.pallas_call(
        feed_forward_kernel,
        grid=(2,),
        in_specs=[whole(128, 2048)] * 4 + [cols(2048, 512), cols(512, 512)],
        out_specs=[cols(512, 512)] * 2
        + [whole(512, 2048)]
        + [whole(128, 2048)] * 4,
        out_shape=[like((512, 1024), BF)] * 2
        + [like((512, 2048), BF)]
        + [like((128, 2048), BF)] * 4,
        scratch_shapes=[pltpu.VMEM((512, 2048), F32), pltpu.VMEM((512, 512), F32)],
        compiler_params=PARAMS,
        cost_estimate=lasts(1),
        name="feed_forward",
    )(*pieces, w_up, d_act)


def weight_kernel(info, *refs, sets, second, unread):
    count = sum(len(entries) + 4 for entries, _ in sets)
    outs, (held, right, total, sems) = refs[:-4], refs[-4:]
    at, first, copies, later, waits = 0, 0, [], [], []
    for j, (entries, width) in enumerate(sets):
        for s in range(4):
            place = right.at[pl.ds(s * 512, 512), pl.ds(first, width)]
            copies.append(pltpu.make_async_copy(refs[at], place, sems.at[at]))
            at += 1
        column = 0
        for entry in entries:
            source = refs[at].at[info[entry]]
            n = source.shape[1]
            for half, into in ((0, copies), (1, later)):
                rows = pl.ds(half * 1024, 1024)
                place = held.at[j, rows, pl.ds(column, n)]
                sem = sems.at[at + half * count]
                into.append(pltpu.make_async_copy(source.at[rows, :], place, sem))
            at, column = at + 1, column + n
        first += width
        waits.append((len(copies), len(later)))
    outs = outs[at + unread :]
    for copy in copies + later:
        copy.start()
    done, first = (0, 0), 0
    for j, (_, width) in enumerate(sets):
        for copy in copies[done[0] : waits[j][0]]:
            copy.wait()
        stop = first + width
        for b in range(4):
            if b == 2:
                for copy in later[done[1] : waits[j][1]]:
                    copy.wait()
            value = dot(held[j, pl.ds(b * 512, 512), :], right[:, first:stop]).astype(BF)
            if second == "z":
                total[:, first:stop] = value
                for s, out in enumerate(outs):
                    rows = pl.ds(pl.multiple_of(info[ORDER_Z + s] * 128, 128), 128)
                    out[pl.ds(b * 128, 128), first:stop] = total[rows, first:stop]
            else:
                for s, out in enumerate(outs):

                    @pl.when(info[REL_Y + b] == s)
                    def _():
                        out[:, first:stop] = value
        done, first = waits[j], stop


def weight_call(info, sets, second, name, others=()):
    operands, known = [], []
    for lefts, rights in sets:
        operands += [*rights, *(x for x, _ in lefts)]
        known.append(([entry for _, entry in lefts], rights[0].shape[1]))
    n = sum(width for _, width in known)
    out_shape = [like((512, n), BF)] * 4
    return pl.pallas_call(
        functools.partial(weight_kernel, sets=known, second=second, unread=len(others)),
        in_specs=[scalars()] + [IN_PLACE] * (len(operands) + len(others)),
        out_specs=[pl.BlockSpec(memory_space=pltpu.VMEM)] * len(out_shape),
        out_shape=out_shape,
        scratch_shapes=[
            pltpu.VMEM((len(sets), 2048, 2048), BF), pltpu.VMEM((2048, n), BF),
            pltpu.VMEM((512, n), BF), pltpu.SemaphoreType.DMA((2 * len(operands),)),
        ],
        compiler_params=PARAMS,
        cost_estimate=lasts(1),
        name=name,
    )(info, *operands, *others)


def output_weight_kernel(info, d0, d1, d2, d3, d4, d5, d6, d7, right, near, *refs):
    out, left = refs[-2:]

    @pl.when(pl.program_id(0) == 0)
    def _():
        for i, piece in enumerate((d0, d1, d2, d3, d4, d5, d6, d7)):
            for j in range(8):
                first = pl.multiple_of(j * 256 + info[PARITY] * 128, 128)
                left[pl.ds(i * 128, 128), pl.ds(j * 128, 128)] = piece[:, pl.ds(first, 128)]

    total = dot_tn(left[:512, :], right[...]) + dot_tn(left[512:, :], near[...])
    out[...] = total.astype(BF)


def output_weight_call(info, grads, rights, others=()):
    return pl.pallas_call(
        output_weight_kernel,
        grid=(2,),
        in_specs=[scalars()] + [whole(128, 2048)] * 8 + [cols(512, 512)] * 2 + [IN_PLACE] * len(others),
        out_specs=cols(1024, 512),
        out_shape=like((1024, 1024), BF),
        scratch_shapes=[pltpu.VMEM((1024, 1024), BF)],
        compiler_params=PARAMS,
        cost_estimate=lasts(1),
        name="output_weights",
    )(info, *grads, *rights, *others)


def sum_kernel(a, b, c, d, *refs):
    value = a[...].astype(F32) + b[...].astype(F32) + c[...].astype(F32) + d[...].astype(F32)
    refs[-1][...] = value.astype(BF)


def sum_call(parts, name, others=()):
    return pl.pallas_call(
        sum_kernel,
        in_specs=[pl.BlockSpec(memory_space=pltpu.VMEM)] * 4 + [IN_PLACE] * len(others),
        out_specs=pl.BlockSpec(memory_space=pltpu.VMEM),
        out_shape=like(parts[0].shape, BF),
        compiler_params=PARAMS,
        cost_estimate=lasts(2),
        name=name,
    )(*parts, *others)


def sum_joined_kernel(parts, out):
    value = parts[0].astype(F32) + parts[1].astype(F32)
    out[...] = value + parts[2].astype(F32) + parts[3].astype(F32)


def sum_joined_call(parts, name):
    return pl.pallas_call(
        sum_joined_kernel,
        out_shape=like(parts.shape[1:], F32),
        compiler_params=PARAMS,
        cost_estimate=lasts(1),
        name=name,
    )(parts)


def widen_kernel(got, query, key, value, gate):
    for i in range(4):
        part = got[2 * i].astype(F32) + got[2 * i + 1].astype(F32)
        wide, narrow = slice(i * 256, (i + 1) * 256), slice(i * 128, (i + 1) * 128)
        gate[:, wide], value[:, wide] = part[:, :256], part[:, 256:512]
        query[:, narrow], key[:, narrow] = part[:, 512:640], part[:, 640:]


def widen_call(got):
    return pl.pallas_call(
        widen_kernel,
        out_shape=[like((64, 512), F32)] * 2 + [like((64, 1024), F32)] * 2,
        compiler_params=PARAMS,
        cost_estimate=lasts(4),
        name="projection_gradients",
    )(got)


def arrived_kernel(*refs):
    refs[-1][...] = jnp.zeros(refs[-1].shape, F32)


def arrived_call(values, name, ahead):
    return pl.pallas_call(
        arrived_kernel,
        in_specs=[IN_PLACE] * len(values),
        out_specs=pl.BlockSpec(memory_space=pltpu.VMEM),
        out_shape=like((8, 128), F32),
        compiler_params=PARAMS,
        cost_estimate=lasts(ahead),
        name=name,
    )(*values)


DP, TENSOR = ("y", "z", "xh"), ("xl", "c")


def shift(value, axis, step):
    return lax.ppermute(value, axis, [(i, (i + step) % 4) for i in range(4)])


def swap(value, axis):
    return lax.ppermute(value, axis, [(0, 1), (1, 0)])


def pair(value, axis):
    return lax.ppermute(value, axis, [(i, i ^ 1) for i in range(4)])


def after(value, *others):
    return lax.optimization_barrier((value,) + others)[0]


def gather_row(own, *held):
    across = swap(own, "xl")
    return [own, across, swap(own, "c"), swap(after(across, *held), "c")]


def scatter_row(parts, hold=None):
    far = add_call(parts[1], swap(parts[3], "c"))
    if hold is not None:
        far = after(far, hold)
    return (parts[0], swap(after(parts[2], far), "c"), swap(far, "xl")), far


def send(values, axis):
    return [shift(v, axis, step) for v, step in zip(values, SHIFTS)]


def exchange(values, axes):
    return lax.all_to_all(values, axes, 0, 0, tiled=True)


def total(values):
    return sum(v.astype(F32) for v in values)


def local(
    tokens,
    segment_ids,
    norm1_gain,
    norm1_shift,
    w_query,
    w_key,
    w_value,
    w_gate,
    w_output,
    norm2_gain,
    norm2_shift,
    w_up,
    w_down,
    cotangent,
):
    info = device_info(
        lax.axis_index("y"), lax.axis_index("z"), lax.axis_index("xl"), lax.axis_index("c")
    )
    seg = segment_ids.reshape(4, 128)
    table = rotation_table()

    pieces = gather_row(after(tokens, info))
    hidden1_t, *saved, gated, p0, p1, p2, p3 = forward_call(
        info, pieces, norm1_gain, norm1_shift, w_query, w_key, w_value, w_gate, w_output, table, seg
    )
    cot = gather_row(after(cotangent, pieces[1]))
    row, sent = scatter_row((p0, p1, p2, after(p3, cot[1])))
    hidden1_y = lax.all_gather(after(hidden1_t, sent), "y")
    cot_all, d_act = cotangent_call((after(cot[0], sent), *cot[1:]), w_down)
    mid_rows, hidden2_rows = middle_call(after(tokens, d_act), row, norm2_gain, norm2_shift)

    gated_near = pair(after(gated, sent), "z")
    hidden2 = gather_row(hidden2_rows, gated_near)
    activated, d_up, hidden2_all, *parts = feed_forward_call(hidden2, w_up, d_act)
    row, sent = scatter_row(parts)
    up_first = row_weight_call(after(hidden2_all, row[1]), after(d_up, row[1]), "y", "up_weights")
    up_part = lax.psum_scatter(after(up_first, row[2]), "y", scatter_dimension=0, tiled=True)
    d_mid, sums2, d_mid_low = norm_back_call(
        row, after(mid_rows, up_first), norm2_gain, cotangent, "second_norm_back", True
    )

    begun = swap(d_mid_low[:16, :128], "c")
    down_first = row_weight_call(after(cot_all, begun), after(activated, begun), "z", "down_weights")
    hidden1_other = swap(after(hidden1_y, d_mid_low), "c")
    d_mid_pieces = gather_row(d_mid_low, down_first)
    near = [pair(d_mid_pieces[0], "z"), pair(d_mid_pieces[1], "z")]
    near += [swap(near[0], "c"), swap(near[1], "c")]
    back = backward_call(
        info, d_mid_pieces, table, seg, after(w_output, hidden1_other), saved,
        w_gate, w_value, w_query, w_key,
    )
    proj_y = [back[0]] + send(back[1:4], "y")
    row, sent = scatter_row((back[4], after(back[5], *near[:2]), *back[6:8]))
    down_part = lax.psum_scatter(after(down_first, sent, up_part), "z", scatter_dimension=0, tiled=True)

    half_x, z = lax.axis_index("xh"), lax.axis_index("z")

    def halves(part, index, move):
        size = part.shape[0] // 2
        mine = lax.dynamic_slice_in_dim(part, index * size, size, 0).astype(F32)
        other = lax.dynamic_slice_in_dim(part, (1 - index) * size, size, 0).astype(BF)
        return mine + move(other).astype(F32)

    def settle(part):
        return halves(part, half_x, lambda other: swap(other, "xh"))

    tokens_grad, sums1 = norm_back_call(row, tokens, norm1_gain, d_mid, "first_norm_back")
    output_first = output_weight_call(info, (*d_mid_pieces, *near), (after(gated, tokens_grad), gated_near))
    output_part = exchange(output_first.reshape(4, 256, 1024), "y")
    output_part = sum_joined_call(output_part.reshape(4, 256, 1024), "output_sum")
    output_half = output_part

    norm_parts = jnp.concatenate([sums1, sums2], axis=0).reshape(4, 128, 16)
    norm_parts = norm_parts.transpose(1, 0, 2).reshape(128, 64)
    norm_got = exchange(norm_parts, DP + TENSOR)
    norm_sums = jnp.sum(norm_got, axis=0).reshape(4, 16)

    sides = [(x, SOURCE_Y + s) for s in range(4) for x in (hidden1_y, hidden1_other)]
    proj_y[0] = after(proj_y[0], tokens_grad)
    proj_parts = weight_call(
        info, [(sides, proj_y)], "z", "projection_weights", (norm_got, arrived_call((*proj_y[1:], output_first), "rows_along_y", 12))
    )
    proj_z = [proj_parts[0]] + send(proj_parts[1:], "z")

    output_part = halves(after(output_part, proj_parts[0]), z // 2, lambda other: shift(other, "z", 2))
    down_part = lax.psum_scatter(down_part, "y", scatter_dimension=0, tiled=True)

    out_parts = down_call(after(activated, proj_parts[0]), w_down)
    row, _ = scatter_row((out_parts[0], after(out_parts[1], proj_parts[0]), *out_parts[2:]))
    block_out = (mid_rows + total(row)).astype(BF)

    ready = sum_call(proj_z, "projection_sum", (output_half,))
    up_part = halves(after(up_part, output_half), z // 2, lambda other: shift(other, "z", 2))
    up_part = halves(up_part, z % 2, lambda other: pair(other, "z"))
    got = exchange(ready.reshape(8, 64, 768), ("y", "xh"))
    query_sum, key_sum, value_sum, gate_sum = widen_call(got)
    return (
        block_out,
        tokens_grad,
        norm_sums[0],
        norm_sums[1],
        query_sum,
        key_sum,
        value_sum,
        gate_sum,
        settle(output_part).T,
        norm_sums[2],
        norm_sums[3],
        settle(up_part),
        settle(down_part).T,
    )


def solution(mesh):
    mesh = Mesh(mesh.devices.reshape(4, 4, 2, 2, 2), DP + TENSOR)
    in_specs = (
        P(DP + TENSOR, None),
        P(DP),
        P(),
        P(),
        P(None, TENSOR),
        P(None, TENSOR),
        P(None, TENSOR),
        P(None, TENSOR),
        P(TENSOR, None),
        P(),
        P(),
        P(None, TENSOR),
        P(TENSOR, None),
        P(DP + TENSOR, None),
    )
    out_specs = (
        P(DP + TENSOR, None),
        P(DP + TENSOR, None),
        P(DP + TENSOR),
        P(DP + TENSOR),
        P(DP, TENSOR),
        P(DP, TENSOR),
        P(DP, TENSOR),
        P(DP, TENSOR),
        P(TENSOR, DP),
        P(DP + TENSOR),
        P(DP + TENSOR),
        P(DP, TENSOR),
        P(TENSOR, DP),
    )
    return jax.shard_map(local, mesh=mesh, in_specs=in_specs, out_specs=out_specs, check_vma=False)
```
